256 devices in a mesh: dp: 4 (over x), psg: 32 (over y, z), tp: 2 (over core).
Axes of the slice: x: 4, y: 4, z: 8, core: 2. Of those that a mesh axis runs over, the one named last changes fastest.
Arguments:
- enc_states: bfloat16 [4, 96, 256, 4096], P('dp', 'psg'), may hold values from -6 to 6
- lengths: int32 [4, 96], P('dp', 'psg'), may hold values from 16 to 256
- enc_gain: bfloat16 [4096], replicated, may hold values from 0.099609375 to 1.8984375
- dec_states: bfloat16 [4, 32, 4096], P('dp'), may hold values from -360 to 360
- w_query: bfloat16 [4096, 2048], P('psg', 'tp'), may hold values from -0.09375 to 0.09375
- w_key: bfloat16 [4096, 2048], P('psg', 'tp'), may hold values from -0.09375 to 0.09375
- w_value: bfloat16 [4096, 2048], P('psg', 'tp'), may hold values from -0.09375 to 0.09375
- w_out: bfloat16 [2048, 4096], P('tp', 'psg'), may hold values from -0.125 to 0.125
Outputs:
- attended: bfloat16 [4, 32, 4096], P('dp', None, 'psg')
- scores: float32 [4, 96], P('dp', 'psg')
The draws below stay inside these ranges and needn't reach their ends.
All inputs are finite; a program needn't handle non-finite values.
Results may differ from the reference program's by a relative error of at most 0.014.
The reference program's roundings to bfloat16 on the way (of `normed`, `queries` and `context`) count: a program that leaves them out, or rounds other values in their place, can miss the bound.
Values may be sent and summed in bfloat16 or wider, within the bound.
No kernel may reach another device: no remote copies, remote signals or barrier semaphores. Data moves between devices by JAX's collectives and lax.ppermute only.
A program may use at most 128 MiB of HBM per device.

```python
import jax
import jax.numpy as jnp
from jax import lax

D = 4096
HEADS = 32
HDIM = 64
PLEN = 256
ANS = 32
QUESTIONS = 4
PASSAGES = 96


def draw_lengths(key, part):
    key = jax.random.fold_in(key, 11)
    first, second = jax.random.split(key)
    lowest = max(1, PLEN // 16)
    drawn = jax.random.randint(first, (QUESTIONS, PASSAGES), lowest, PLEN + 1)
    chosen = jax.random.randint(second, (QUESTIONS, 1), 0, PASSAGES)
    where_full = jnp.arange(PASSAGES, dtype=jnp.int32)[None, :] == chosen
    return jnp.where(where_full, PLEN, drawn).astype(jnp.int32)


def draw_dec_states(key, part):
    key = jax.random.fold_in(key, 23)
    first = jax.random.fold_in(key, 0)
    base = jnp.clip(jax.random.normal(first, (QUESTIONS, ANS, D), jnp.float32), -6.0, 6.0)
    return base.astype(jnp.bfloat16)


def levels(key, extent, cuts, least, top_value):
    loudness = 1.0
    for axis_at, shards_of in cuts:
        steps = jax.random.uniform(jax.random.fold_in(jax.random.fold_in(key, 6), axis_at), (shards_of,), jnp.float32, least / len(cuts), top_value / len(cuts))
        loudness = loudness * jnp.repeat(jnp.exp(steps), extent[axis_at] // shards_of).reshape((-1,) + (1,) * (len(extent) - 1 - axis_at))
    return loudness


def gaussian(key, extent, width, bound, cuts=(), kind=jnp.bfloat16):
    values = jax.random.normal(key, extent, jnp.float32) * width
    if len(cuts) > 0:
        values = levels(key, extent, cuts, -0.22, 0.18) * values
    return jnp.clip(values, min=-bound, max=bound).astype(kind)


def setup_inputs(seed: int = 0) -> dict:
    key_list = jax.random.split(jax.random.key(seed), 9)
    return {
        "enc_states": gaussian(key_list[0], (QUESTIONS, PASSAGES, PLEN, D), 1.0, 6.0, ((0, 4), (1, 32))),
        "lengths": draw_lengths(jax.random.fold_in(key_list[8], 71), 0),
        "enc_gain": jnp.clip(1.0 + 0.18 * jax.random.normal(key_list[2], (D,), jnp.float32), 0.099609375, 1.8984375).astype(jnp.bfloat16),
        "dec_states": draw_dec_states(jax.random.fold_in(key_list[8], 71), 0),
        "w_query": gaussian(key_list[4], (D, HEADS * HDIM), D ** -0.5, 0.09375, ((0, 32), (1, 2))),
        "w_key": gaussian(key_list[5], (D, HEADS * HDIM), D ** -0.5, 0.09375, ((0, 32), (1, 2))),
        "w_value": gaussian(key_list[6], (D, HEADS * HDIM), D ** -0.5, 0.09375, ((0, 32), (1, 2))),
        "w_out": gaussian(key_list[7], (HEADS * HDIM, D), (HEADS * HDIM) ** -0.5, 0.125, ((0, 2), (1, 32))),
    }


def one_question(items, enc_gain, w_query, w_key, w_value, w_out):
    enc, lens, dec = items
    e32 = enc.astype(jnp.float32)
    scale = lax.rsqrt(lax.optimization_barrier(jnp.mean(e32 * e32, axis=-1, keepdims=True)) + 1e-06)
    normed = (e32 * scale * enc_gain.astype(jnp.float32)).astype(jnp.bfloat16)
    normed = normed.reshape(PASSAGES * PLEN, D)
    keys = jnp.dot(normed, w_key, preferred_element_type=jnp.float32).astype(jnp.bfloat16)
    values = jnp.dot(normed, w_value, preferred_element_type=jnp.float32).astype(jnp.bfloat16)
    queries = jnp.dot(dec, w_query, preferred_element_type=jnp.float32).astype(jnp.bfloat16)
    keys = keys.reshape(PASSAGES * PLEN, HEADS, HDIM).astype(jnp.float32)
    values = values.reshape(PASSAGES * PLEN, HEADS, HDIM).astype(jnp.float32)
    queries = queries.reshape(ANS, HEADS, HDIM).astype(jnp.float32)
    logits = jnp.einsum('ahe,khe->hak', queries, keys) * HDIM ** (-0.5)
    valid = (jnp.arange(PLEN, dtype=jnp.int32)[None, :] < lens[:, None]).reshape(PASSAGES * PLEN)
    masked = jnp.where(valid[None, None, :], logits, -1e+30)
    top = lax.optimization_barrier(jnp.max(masked, axis=-1, keepdims=True))
    weights = jnp.where(valid[None, None, :], jnp.exp(masked - top), 0.0)
    total = lax.optimization_barrier(jnp.sum(weights, axis=-1))
    numer = jnp.einsum('hak,khe->ahe', weights, values)
    context = (numer / jnp.transpose(total)[:, :, None]).astype(jnp.bfloat16)
    attended = jnp.dot(context.reshape(ANS, HEADS * HDIM), w_out, preferred_element_type=jnp.float32).astype(jnp.bfloat16)
    share = weights / total[:, :, None]
    mass = lax.optimization_barrier(jnp.sum(share.reshape(HEADS, ANS, PASSAGES, PLEN), axis=(0, 1, 3)))
    scores = mass * (PASSAGES / (HEADS * ANS))
    return (attended, scores)

def reference(enc_states, lengths, enc_gain, dec_states, w_query, w_key, w_value, w_out):

    def step(items):
        return one_question(items, enc_gain, w_query, w_key, w_value, w_out)
    attended, scores = lax.map(step, (enc_states, lengths, dec_states))
    return (attended, scores)
```

```python
import functools

import jax
import jax.numpy as jnp
from jax import lax
from jax.experimental import pallas as pl
from jax.experimental.pallas import tpu as pltpu
from jax.sharding import Mesh, PartitionSpec as P

HEADS = 32
HDIM = 64
NX = 4
NY = 4
NZ = 8
LANES = 128
PSG = ("y", "z")
SIZES = {"dp": NX, "y": NY, "z": NZ}
VMEM = pl.BlockSpec(memory_space=pltpu.VMEM)
SMEM = pl.BlockSpec(memory_space=pltpu.SMEM)
HBM = pl.BlockSpec(memory_space=pltpu.HBM)
f32 = jnp.float32
bf16 = jnp.bfloat16

GROUPS = ((0, 1, 7), (2, 6, 3, 5, 4))
ORDER = [(dy, dz) for group in GROUPS for dz in group for dy in range(NY)]


def shaped(shape, dtype=f32):
    return jax.ShapeDtypeStruct(shape, dtype)


def params(mib):
    return pltpu.CompilerParams(vmem_limit_bytes=mib * 1024 * 1024)


def call(kernel, outs, scratch, *args, mib=16, flops=0, hbm=()):
    specs = [SMEM] + [HBM if i in hbm else VMEM for i in range(1, len(args))]
    return pl.pallas_call(
        kernel,
        out_shape=outs,
        in_specs=specs,
        out_specs=jax.tree.map(lambda _: VMEM, outs),
        scratch_shapes=scratch,
        compiler_params=params(mib),
        cost_estimate=pl.CostEstimate(flops=flops, bytes_accessed=1 << 20, transcendentals=0),
    )(*args)


def recv(a, axis, k):
    n = SIZES[axis]
    return lax.ppermute(a, axis, [((i + k) % n, i) for i in range(n)])


def exchange(a):
    return lax.all_to_all(a, PSG, split_axis=0, concat_axis=0, tiled=True)


def round_x(group):
    half = group.shape[0] // 2
    up, down = recv(group, "dp", 1), recv(group, "dp", -1)
    far = [recv(up[:half], "dp", 1), recv(down[half:], "dp", -1)]
    return [[group], [up], far, [down]]


def gather(shard):
    block = jnp.concatenate(
        [shard, recv(shard, "y", 1), recv(shard, "y", 2), recv(shard, "y", -1)], axis=0
    )
    half = block.shape[0] // 2
    up1, down1 = recv(block, "z", 1), recv(block, "z", -1)
    near = round_x(jnp.concatenate([block, up1, down1], axis=0))
    up2, down2 = recv(up1, "z", 1), recv(down1, "z", -1)
    up3, down3 = recv(up2, "z", 1), recv(down2, "z", -1)
    after = (near[1][0][0, 0] + near[3][0][0, 0]) * 0
    far = (recv(up3[:half] + after, "z", 1), recv(down3[half:] + after, "z", -1))
    rest = round_x(jnp.concatenate([up2, down2, up3, down3, *far], axis=0))
    return [near[dx] + rest[dx] for dx in range(NX)]


def norm_kernel(pos, e_ref, gain_ref, plain_ref, turned_ref):
    e = e_ref[...].astype(f32)
    scale = lax.rsqrt(jnp.mean(e * e, axis=-1, keepdims=True) + 1e-06)
    plain_ref[...] = (e * scale * gain_ref[...].astype(f32)).astype(bf16)
    for i, (dy, dz) in enumerate(ORDER):
        at = lax.rem(pos[0] + dy, NY) * NZ + lax.rem(pos[1] + dz, NZ)
        turned_ref[:, i * LANES : (i + 1) * LANES] = plain_ref[
            :, pl.ds(pl.multiple_of(at * LANES, LANES), LANES)
        ]


def normalise(pos, enc, gain, tile):
    rows, width = enc.shape
    block = pl.BlockSpec((tile, width), lambda i, pos: (i, 0))
    return pl.pallas_call(
        norm_kernel,
        out_shape=[shaped((rows, width), bf16)] * 2,
        grid_spec=pltpu.PrefetchScalarGridSpec(
            num_scalar_prefetch=1,
            grid=(rows // tile,),
            in_specs=[block, pl.BlockSpec((1, width), lambda i, pos: (0, 0))],
            out_specs=[block, block],
        ),
        compiler_params=params(32),
        cost_estimate=pl.CostEstimate(
            flops=6 * rows * width, bytes_accessed=6 * rows * width, transcendentals=0
        ),
    )(pos, enc, gain)


def project_kernel(x_ref, *refs):
    pieces, out_ref = refs[:-1], refs[-1]
    acc, at = None, 0
    for ref in pieces:
        depth = ref.shape[0]
        part = jnp.dot(x_ref[:, at : at + depth], ref[...], preferred_element_type=f32)
        acc = part if acc is None else acc + part
        at += depth
    out_ref[...] = acc.astype(bf16)


def project(x, pieces):
    rows, width = x.shape
    cols = pieces[0].shape[1]
    return pl.pallas_call(
        project_kernel,
        out_shape=shaped((rows, cols), bf16),
        in_specs=[VMEM] * (1 + len(pieces)),
        out_specs=VMEM,
        compiler_params=params(16),
        cost_estimate=pl.CostEstimate(
            flops=2 * rows * width * cols,
            bytes_accessed=2 * (rows * width + width * cols + rows * cols),
            transcendentals=0,
        ),
    )(x, *pieces)


def query_kernel(pos, dec_ref, w_ref, out_ref):
    at = pl.multiple_of((pos[0] * NZ + pos[1]) * LANES, LANES)
    part = jnp.dot(dec_ref[:, pl.ds(at, LANES)], w_ref[...], preferred_element_type=f32)
    for j in range(out_ref.shape[1]):
        out_ref[:, j, :] = part[:, j * LANES : (j + 1) * LANES]


def spread_kernel(pos, got_ref, out_ref):
    total = jnp.sum(got_ref[...], axis=0, keepdims=True)
    out_ref[...] = jnp.broadcast_to(total, out_ref.shape)


def summed(pos, parts):
    return exchange(call(spread_kernel, shaped(parts.shape), [], pos, exchange(parts)))


def same_head(rows, cols, answers):
    row = lax.broadcasted_iota(jnp.int32, (rows, cols), 0) // answers
    col = lax.broadcasted_iota(jnp.int32, (rows, cols), 1) // HDIM
    return row == col


def logits_kernel(plen, pos, q_ref, *refs):
    keys, (high_ref, low_ref, stat_ref, copies_ref, tile_ref) = refs[:NX], refs[NX:]
    answers = q_ref.shape[0]
    for dx, key_ref in enumerate(keys):
        quarter = lax.rem(pos[2] + dx, NX)
        slots, cols = key_ref.shape
        pairs = cols // HDIM * answers
        blocks = cols // LANES
        q = jnp.concatenate(
            [q_ref[:, pl.ds(quarter * blocks + j, 1), :].reshape(answers, LANES) for j in range(blocks)],
            axis=1,
        )
        spread = jnp.where(
            same_head(pairs, cols, answers), jnp.concatenate([q] * (cols // HDIM), axis=0), 0.0
        ).astype(bf16)
        logits = lax.dot_general(
            spread, key_ref[...], (((1,), (1,)), ((), ())), preferred_element_type=f32
        ) * HDIM ** (-0.5)
        token = lax.broadcasted_iota(jnp.int32, (pairs, plen), 1)
        passages = slots // plen
        valid = [token < pos[3 + i] for i in range(passages)]
        masked = [
            jnp.where(valid[i], logits[:, i * plen : (i + 1) * plen], -1e30) for i in range(passages)
        ]
        top = functools.reduce(
            jnp.maximum, [jnp.max(m, axis=1, keepdims=True) for m in masked]
        )
        at = pl.ds(pl.multiple_of(quarter * pairs, pairs), pairs)
        lane = lax.broadcasted_iota(jnp.int32, (pairs, LANES), 1)
        tile = jnp.where(lane == 0, top, 0.0)
        total = jnp.zeros_like(top)
        for i in range(passages):
            p = jnp.where(valid[i], jnp.exp(masked[i] - top), 0.0)
            high = p.astype(bf16)
            high_ref[at, i * plen : (i + 1) * plen] = high
            low_ref[at, i * plen : (i + 1) * plen] = (p - high.astype(f32)).astype(bf16)
            part = jnp.sum(p, axis=1, keepdims=True)
            total = total + part
            tile = jnp.where(lane == 2 + i, part, tile)
        tile_ref[at, :] = jnp.where(lane == 1, total, tile)
    stat_ref[...] = jnp.transpose(tile_ref[...])[0:8, :]
    copies_ref[...] = jnp.broadcast_to(stat_ref[0:2, :][None], copies_ref.shape)


def weigh_kernel(high_ref, low_ref, x_ref, u_ref):
    total = jnp.dot(high_ref[...], x_ref[...], preferred_element_type=f32)
    total += jnp.dot(low_ref[...], x_ref[...], preferred_element_type=f32)
    high = total.astype(bf16)
    low = (total - high.astype(f32)).astype(bf16)
    per = total.shape[0] // NX
    for g in range(NX):
        at = slice(g * per, (g + 1) * per)
        u_ref[2 * g * per : (2 * g + 1) * per, :] = high[at, :]
        u_ref[(2 * g + 1) * per : (2 * g + 2) * per, :] = low[at, :]


def weigh(high, low, x, tile):
    pairs, slots = high.shape
    width = x.shape[1]
    whole = pl.BlockSpec((pairs, slots), lambda i: (0, 0))
    return pl.pallas_call(
        weigh_kernel,
        out_shape=shaped((2 * pairs, width), bf16),
        grid=(width // tile,),
        in_specs=[whole, whole, pl.BlockSpec((slots, tile), lambda i: (0, i))],
        out_specs=pl.BlockSpec((2 * pairs, tile), lambda i: (0, i)),
        compiler_params=params(24),
        cost_estimate=pl.CostEstimate(
            flops=4 * pairs * slots * width, bytes_accessed=1 << 24, transcendentals=0
        ),
    )(high, low, x)


def numer_kernel(pos, own_ref, stats_ref, u_ref, v_hbm, out_ref, mass_ref, buf, acc, sems):
    chunks, depth, columns = buf.shape
    answers = out_ref.shape[0]
    cols = columns // NX
    per = u_ref.shape[0] // NX

    def fetch(i):
        return pltpu.make_async_copy(v_hbm.at[pl.ds(i * depth, depth), :], buf.at[i], sems.at[i])

    for i in range(chunks):
        fetch(i).start()
    tops = stats_ref[:, 0, :]
    top = jnp.max(tops, axis=0, keepdims=True)
    total = jnp.sum(stats_ref[:, 1, :] * jnp.exp(tops - top), axis=0, keepdims=True)
    factor = jnp.exp(own_ref[0:1, :] - top) / total
    for i in range(8):
        part = jnp.sum(own_ref[2 + i : 3 + i, :] * factor, keepdims=True) if i < 6 else 0.0
        mass_ref[i : i + 1, :] = jnp.broadcast_to(part, (1, LANES))
    column = jnp.transpose(jnp.broadcast_to(factor, (LANES, factor.shape[1])))
    for i in range(chunks):
        fetch(i).wait()
        for g in range(NX):
            part = jnp.dot(
                u_ref[g * per : (g + 1) * per, i * depth : (i + 1) * depth],
                buf[i, :, g * cols : (g + 1) * cols],
                preferred_element_type=f32,
            )
            acc[g] = part if i == 0 else acc[g] + part
    pairs = per // 2
    for g in range(NX):
        numer = acc[g, :pairs, :] + acc[g, pairs:, :]
        scaled = column[g * pairs : (g + 1) * pairs, :]
        numer = numer * jnp.concatenate([scaled] * (cols // LANES), axis=1)
        numer = jnp.where(same_head(pairs, cols, answers), numer, 0.0)
        rows = numer[0:answers, :]
        for h in range(1, pairs // answers):
            rows = rows + numer[h * answers : (h + 1) * answers, :]
        for j in range(cols // LANES):
            out_ref[:, g * (cols // LANES) + j, :] = rows[:, j * LANES : (j + 1) * LANES]


def out_kernel(pos, ctx_ref, mass_ref, w_ref, out_ref):
    answers, blocks, _ = ctx_ref.shape
    ctx = jnp.concatenate([ctx_ref[:, j, :] for j in range(blocks)], axis=1).astype(bf16)
    out_ref[0:answers, :] = jnp.dot(ctx, w_ref[...], preferred_element_type=f32)
    out_ref[answers : answers + 8, :] = mass_ref[...]


def body(enc_states, lengths, enc_gain, dec_states, w_query, w_key, w_value, w_out):
    qdev, pdev, plen, width = enc_states.shape
    answers = dec_states.shape[1]
    columns = w_key.shape[1]
    pairs = columns // HDIM * answers
    slots = pdev * plen
    quarter = columns // NX
    blocks = columns // LANES
    members = NY * NZ
    x, y, z = (lax.axis_index(axis).astype(jnp.int32) for axis in ("dp", "y", "z"))
    pos = jnp.concatenate([jnp.stack([y, z, x]), lengths.reshape(pdev)])

    values = lax.all_gather(w_value, PSG, axis=0, tiled=True)
    mine = lax.dynamic_slice(w_key, (0, x * quarter), (w_key.shape[0], quarter))
    key_blocks = gather(mine)

    q_parts = call(
        query_kernel,
        shaped((answers, blocks, LANES)),
        [],
        pos,
        dec_states.reshape(answers, width),
        w_query,
    )
    queries = summed(pos, q_parts)

    plain, turned = normalise(pos, enc_states.reshape(slots, width), enc_gain[None], plen)
    keys = [project(turned, pieces) for pieces in key_blocks]
    high, low, stat, copies = call(
        functools.partial(logits_kernel, plen),
        [
            shaped((pairs, slots), bf16),
            shaped((pairs, slots), bf16),
            shaped((8, pairs)),
            shaped((members, 2, pairs)),
        ],
        [pltpu.VMEM((pairs, LANES), f32)],
        pos,
        queries,
        *keys,
    )
    stats = exchange(copies)
    weighed = weigh(high, low, plain, 512)
    chunks = 8
    parts, mass = call(
        numer_kernel,
        [shaped((answers, blocks, LANES)), shaped((8, LANES))],
        [
            pltpu.VMEM((chunks, width // chunks, columns), bf16),
            pltpu.VMEM((NX, 2 * pairs // NX, quarter), f32),
            pltpu.SemaphoreType.DMA((chunks,)),
        ],
        pos,
        stat,
        stats,
        weighed,
        values,
        mib=46,
        flops=4 * pairs * width * quarter,
        hbm=(4,),
    )
    context = summed(pos, parts)
    part = call(out_kernel, shaped((answers + 8, w_out.shape[1])), [], pos, context, mass, w_out)
    both = part + lax.ppermute(part, "tp", [(0, 1), (1, 0)])
    scores = both[answers : answers + pdev, 0] * (pdev * members / (HEADS * answers))
    return both[:answers].astype(bf16)[None], scores[None]


def solution(mesh):
    fine = Mesh(mesh.devices.reshape(NX, NY, NZ, 2), ("dp", "y", "z", "tp"))
    placed = (
        P("dp", PSG, None, None),
        P("dp", PSG),
        P(),
        P("dp", None, None),
        P(PSG, "tp"),
        P(PSG, "tp"),
        P(PSG, "tp"),
        P("tp", PSG),
    )
    return jax.shard_map(
        body,
        mesh=fine,
        in_specs=placed,
        out_specs=(P("dp", None, PSG), P("dp", PSG)),
        check_vma=False,
    )
```

```python
import functools

import jax
import jax.numpy as jnp
from jax import lax
from jax.experimental import pallas as pl
from jax.experimental.pallas import tpu as pltpu
from jax.sharding import Mesh, PartitionSpec as P

HEADS = 32
HDIM = 64
NX = 4
NY = 4
NZ = 8
LANES = 128
PSG = ("y", "z")
SIZES = {"dp": NX, "y": NY, "z": NZ}
VMEM = pl.BlockSpec(memory_space=pltpu.VMEM)
SMEM = pl.BlockSpec(memory_space=pltpu.SMEM)
f32 = jnp.float32
bf16 = jnp.bfloat16

GROUPS = ((0, 1, 7), (2, 6, 3, 5, 4))
ORDER = [(dy, dz) for group in GROUPS for dz in group for dy in range(NY)]


def shaped(shape, dtype=f32):
    return jax.ShapeDtypeStruct(shape, dtype)


def params(mib):
    return pltpu.CompilerParams(vmem_limit_bytes=mib * 1024 * 1024)


def call(kernel, outs, scratch, *args, mib=16, flops=0):
    specs = [SMEM] + [VMEM] * (len(args) - 1)
    return pl.pallas_call(
        kernel,
        out_shape=outs,
        in_specs=specs,
        out_specs=jax.tree.map(lambda _: VMEM, outs),
        scratch_shapes=scratch,
        compiler_params=params(mib),
        cost_estimate=pl.CostEstimate(flops=flops, bytes_accessed=1 << 20, transcendentals=0),
    )(*args)


def recv(a, axis, k):
    n = SIZES[axis]
    return lax.ppermute(a, axis, [((i + k) % n, i) for i in range(n)])


def exchange(a):
    return lax.all_to_all(a, PSG, split_axis=0, concat_axis=0, tiled=True)


def round_x(group, after):
    half = group.shape[0] // 2
    up, down = recv(group, "dp", 1), recv(group, "dp", -1)
    far = [recv(up[:half] + after, "dp", 1), recv(down[half:] + after, "dp", -1)]
    return [[group], [up], far, [down]]


def first_of(*arrays):
    return sum(a[(0,) * a.ndim].astype(bf16) for a in arrays) * 0


def gather(shard, after):
    block = jnp.concatenate(
        [shard, recv(shard, "y", 1), recv(shard, "y", 2), recv(shard, "y", -1)], axis=0
    )
    half = block.shape[0] // 2
    up1, down1 = recv(block, "z", 1), recv(block, "z", -1)
    near = round_x(jnp.concatenate([block, up1, down1], axis=0), 0)
    up2, down2 = recv(up1, "z", 1), recv(down1, "z", -1)
    up3, down3 = recv(up2, "z", 1), recv(down2, "z", -1)
    last = first_of(*near[2])
    far = (recv(up3[:half], "z", 1) + last, recv(down3[half:], "z", -1) + last)
    rest = round_x(jnp.concatenate([up2, down2, up3, down3, *far], axis=0), after)
    return [near[dx] + rest[dx] for dx in range(NX)]


def norm_kernel(pos, e_ref, gain_ref, plain_ref, turned_ref):
    e = e_ref[...].astype(f32)
    scale = lax.rsqrt(jnp.mean(e * e, axis=-1, keepdims=True) + 1e-06)
    plain_ref[...] = (e * scale * gain_ref[...].astype(f32)).astype(bf16)
    for i, (dy, dz) in enumerate(ORDER):
        at = lax.rem(pos[0] + dy, NY) * NZ + lax.rem(pos[1] + dz, NZ)
        turned_ref[:, i * LANES : (i + 1) * LANES] = plain_ref[
            :, pl.ds(pl.multiple_of(at * LANES, LANES), LANES)
        ]


def normalise(pos, enc, gain, tile):
    rows, width = enc.shape
    block = pl.BlockSpec((tile, width), lambda i, pos: (i, 0))
    return pl.pallas_call(
        norm_kernel,
        out_shape=[shaped((rows, width), bf16)] * 2,
        grid_spec=pltpu.PrefetchScalarGridSpec(
            num_scalar_prefetch=1,
            grid=(rows // tile,),
            in_specs=[block, pl.BlockSpec((1, width), lambda i, pos: (0, 0))],
            out_specs=[block, block],
        ),
        compiler_params=params(32),
        cost_estimate=pl.CostEstimate(
            flops=6 * rows * width, bytes_accessed=6 * rows * width, transcendentals=0
        ),
    )(pos, enc, gain)


def project_kernel(x_ref, *refs):
    pieces, out_ref = refs[:-1], refs[-1]
    tile = min(out_ref.shape[1], 256)
    for col in range(0, out_ref.shape[1], tile):
        acc, at = None, 0
        for ref in pieces:
            depth = ref.shape[0]
            part = jnp.dot(
                x_ref[:, at : at + depth], ref[:, col : col + tile], preferred_element_type=f32
            )
            acc = part if acc is None else acc + part
            at += depth
        out_ref[:, col : col + tile] = acc.astype(bf16)


def project(x, pieces):
    rows, width = x.shape
    cols = pieces[0].shape[1]
    return pl.pallas_call(
        project_kernel,
        out_shape=shaped((rows, cols), bf16),
        in_specs=[VMEM] * (1 + len(pieces)),
        out_specs=VMEM,
        compiler_params=params(16),
        cost_estimate=pl.CostEstimate(
            flops=2 * rows * width * cols,
            bytes_accessed=2 * (rows * width + width * cols + rows * cols),
            transcendentals=0,
        ),
    )(x, *pieces)


def query_kernel(pos, dec_ref, w_ref, out_ref):
    at = pl.multiple_of((pos[0] * NZ + pos[1]) * LANES, LANES)
    part = jnp.dot(dec_ref[:, pl.ds(at, LANES)], w_ref[...], preferred_element_type=f32)
    for j in range(out_ref.shape[1]):
        out_ref[:, j, :] = part[:, j * LANES : (j + 1) * LANES]


def spread_kernel(pos, got_ref, out_ref):
    total = jnp.sum(got_ref[...], axis=0, keepdims=True)
    out_ref[...] = jnp.broadcast_to(total, out_ref.shape)


def same_head(rows, cols, answers):
    row = lax.broadcasted_iota(jnp.int32, (rows, cols), 0) // answers
    col = lax.broadcasted_iota(jnp.int32, (rows, cols), 1) // HDIM
    return row == col


def attend_kernel(plen, pos, q_ref, v_ref, *refs):
    keys, (out_ref, mass_ref) = refs[:NX], refs[NX:]
    answers = q_ref.shape[0]
    lane = lax.broadcasted_iota(jnp.int32, (answers, LANES), 1)
    last = out_ref.shape[1] - 1
    stats = jnp.zeros((answers, LANES), f32)
    passages = v_ref.shape[0] // plen
    masses = [stats] * passages
    for dx, key_ref in enumerate(keys):
        quarter = lax.rem(pos[2] + dx, NX)
        slots, cols = key_ref.shape
        heads = cols // HDIM
        pairs = heads * answers
        blocks = cols // LANES
        q = jnp.concatenate(
            [q_ref[:, pl.ds(quarter * blocks + j, 1), :].reshape(answers, LANES) for j in range(blocks)],
            axis=1,
        )
        own = same_head(pairs, cols, answers)
        spread = jnp.where(own, jnp.concatenate([q] * heads, axis=0), 0.0).astype(bf16)
        logits = lax.dot_general(
            spread, key_ref[...], (((1,), (1,)), ((), ())), preferred_element_type=f32
        ) * HDIM ** (-0.5)
        token = lax.broadcasted_iota(jnp.int32, (pairs, plen), 1)
        valid = [token < pos[3 + i] for i in range(passages)]
        masked = [
            jnp.where(valid[i], logits[:, i * plen : (i + 1) * plen], -1e30) for i in range(passages)
        ]
        top = functools.reduce(jnp.maximum, [jnp.max(m, axis=1, keepdims=True) for m in masked])
        p = [jnp.where(valid[i], jnp.exp(masked[i] - top), 0.0) for i in range(passages)]
        sums = [jnp.sum(part, axis=1, keepdims=True) for part in p]
        total = functools.reduce(jnp.add, sums)
        for h in range(heads):
            at = slice(h * answers, (h + 1) * answers)
            head = quarter * heads + h
            stats = jnp.where(lane == head, top[at, :], stats)
            stats = jnp.where(lane == head + LANES // 2, total[at, :], stats)
            masses = [jnp.where(lane == head, s[at, :], m) for s, m in zip(sums, masses)]
        whole = jnp.concatenate(p, axis=1)
        high = whole.astype(bf16)
        low = (whole - high.astype(f32)).astype(bf16)
        v = v_ref[:, pl.ds(pl.multiple_of(quarter * cols, cols), cols)]
        numer = jnp.dot(high, v, preferred_element_type=f32)
        numer += jnp.dot(low, v, preferred_element_type=f32)
        numer = jnp.where(own, numer, 0.0)
        rows = numer[0:answers, :]
        for h in range(1, heads):
            rows = rows + numer[h * answers : (h + 1) * answers, :]
        for j in range(blocks):
            out_ref[:, pl.ds(quarter * blocks + j, 1), :] = rows[
                :, j * LANES : (j + 1) * LANES
            ].reshape(answers, 1, LANES)
    out_ref[:, last, :] = stats
    for i, mass in enumerate(masses):
        mass_ref[i] = mass


def by_head(lane, row, j):
    return jnp.where(lane < HDIM, row[:, 2 * j : 2 * j + 1], row[:, 2 * j + 1 : 2 * j + 2])


def merge_kernel(pos, got_ref, out_ref):
    last = got_ref.shape[1] - 1
    stats = got_ref[:, last, :]
    top = jnp.max(stats, axis=0, keepdims=True)
    scale = jnp.exp(stats - top)
    total = jnp.sum(pltpu.roll(stats, LANES // 2, 1) * scale, axis=0, keepdims=True)
    lane = lax.broadcasted_iota(jnp.int32, scale.shape, 1)
    first = lane[0:1, :]
    for j in range(last):
        numer = jnp.sum(got_ref[:, j, :] * by_head(lane, scale, j), axis=0, keepdims=True)
        row = numer / by_head(first, total, j)
        out_ref[:, j, :] = jnp.broadcast_to(row, scale.shape)
    row = jnp.where(first < LANES // 2, top, pltpu.roll(total, LANES // 2, 1))
    out_ref[:, last, :] = jnp.broadcast_to(row, scale.shape)


def out_kernel(pos, ctx_ref, parts_ref, mass_ref, w_ref, out_ref):
    answers, rows, _ = ctx_ref.shape
    last = rows - 1
    ctx = jnp.concatenate([ctx_ref[:, j, :] for j in range(last)], axis=1).astype(bf16)
    out_ref[0:answers, :] = jnp.dot(ctx, w_ref[...], preferred_element_type=f32)
    merged = ctx_ref[:, last, :]
    lane = lax.broadcasted_iota(jnp.int32, merged.shape, 1)
    heads = last * LANES // HDIM
    total = jnp.where(lane < heads, pltpu.roll(merged, LANES // 2, 1), 1.0)
    gap = jnp.where(lane < heads, parts_ref[:, last, :] - merged, 0.0)
    factor = jnp.exp(gap) / total
    for i in range(8):
        part = jnp.sum(mass_ref[i] * factor, keepdims=True) if i < mass_ref.shape[0] else 0.0
        out_ref[answers + i : answers + i + 1, :] = jnp.broadcast_to(part, (1, LANES))


def body(enc_states, lengths, enc_gain, dec_states, w_query, w_key, w_value, w_out):
    qdev, pdev, plen, width = enc_states.shape
    answers = dec_states.shape[1]
    columns = w_key.shape[1]
    pairs = columns // HDIM * answers
    slots = pdev * plen
    quarter = columns // NX
    blocks = columns // LANES
    members = NY * NZ
    x, y, z = (lax.axis_index(axis).astype(jnp.int32) for axis in ("dp", "y", "z"))
    pos = jnp.concatenate([jnp.stack([y, z, x]), lengths.reshape(pdev)])

    w_values = lax.all_gather(w_value, PSG, axis=0, tiled=True)
    plain, turned = normalise(pos, enc_states.reshape(slots, width), enc_gain[None], plen)
    q_parts = call(
        query_kernel,
        shaped((answers, blocks, LANES)),
        [],
        pos,
        dec_states.reshape(answers, width),
        w_query,
    )
    q_sum = call(spread_kernel, shaped(q_parts.shape), [], pos, exchange(q_parts))
    queries = exchange(q_sum)

    mine = lax.dynamic_slice(w_key, (0, x * quarter), (w_key.shape[0], quarter))
    keys = [project(turned, pieces) for pieces in gather(mine, first_of(plain))]
    values = project(plain, [w_values])
    parts, mass = call(
        functools.partial(attend_kernel, plen),
        [shaped((answers, blocks + 1, LANES)), shaped((pdev, answers, LANES))],
        [],
        pos,
        queries,
        values,
        *keys,
        flops=4 * pairs * slots * quarter * 2,
    )
    merged = call(merge_kernel, shaped(parts.shape), [], pos, exchange(parts))
    context = exchange(merged)
    part = call(
        out_kernel, shaped((answers + 8, w_out.shape[1])), [], pos, context, parts, mass, w_out
    )
    both = part + lax.ppermute(part, "tp", [(0, 1), (1, 0)])
    scores = both[answers : answers + pdev, 0] * (pdev * members / (HEADS * answers))
    return both[:answers].astype(bf16)[None], scores[None]


def solution(mesh):
    fine = Mesh(mesh.devices.reshape(NX, NY, NZ, 2), ("dp", "y", "z", "tp"))
    placed = (
        P("dp", PSG, None, None),
        P("dp", PSG),
        P(),
        P("dp", None, None),
        P(PSG, "tp"),
        P(PSG, "tp"),
        P(PSG, "tp"),
        P("tp", PSG),
    )
    return jax.shard_map(
        body,
        mesh=fine,
        in_specs=placed,
        out_specs=(P("dp", None, PSG), P("dp", PSG)),
        check_vma=False,
    )
```

```python
import functools

import jax
import jax.numpy as jnp
from jax import lax
from jax.experimental import pallas as pl
from jax.experimental.pallas import tpu as pltpu
from jax.sharding import Mesh, PartitionSpec as P

HEADS = 32
HDIM = 64
NX = 4
NY = 4
NZ = 8
LANES = 128
PSG = ("y", "z")
SIZES = {"dp": NX, "y": NY, "z": NZ}
VMEM = pl.BlockSpec(memory_space=pltpu.VMEM)
SMEM = pl.BlockSpec(memory_space=pltpu.SMEM)
HBM = pl.BlockSpec(memory_space=pltpu.HBM)
f32 = jnp.float32
bf16 = jnp.bfloat16

GROUPS = ((0, 1, 7), (2, 6, 3, 5, 4))
ORDER = [(dy, dz) for group in GROUPS for dz in group for dy in range(NY)]


def shaped(shape, dtype=f32):
    return jax.ShapeDtypeStruct(shape, dtype)


def params(mib):
    return pltpu.CompilerParams(vmem_limit_bytes=mib * 1024 * 1024)


def call(kernel, outs, scratch, *args, mib=8, flops=0, hbm=()):
    specs = [SMEM] + [HBM if i in hbm else VMEM for i in range(1, len(args))]
    return pl.pallas_call(
        kernel,
        out_shape=outs,
        in_specs=specs,
        out_specs=jax.tree.map(lambda _: VMEM, outs),
        scratch_shapes=scratch,
        compiler_params=params(mib),
        cost_estimate=pl.CostEstimate(flops=flops, bytes_accessed=1 << 20, transcendentals=0),
    )(*args)


def recv(a, axis, k):
    n = SIZES[axis]
    return lax.ppermute(a, axis, [((i + k) % n, i) for i in range(n)])


def exchange(a):
    return lax.all_to_all(a, PSG, split_axis=0, concat_axis=0, tiled=True)


def round_x(group, after):
    half = group.shape[0] // 2
    up, down = recv(group, "dp", 1), recv(group, "dp", -1)
    far = [recv(up[:half] + after, "dp", 1), recv(down[half:] + after, "dp", -1)]
    return [[group], [up], far, [down]]


def first_of(*arrays):
    return sum(a[(0,) * a.ndim].astype(bf16) for a in arrays) * 0


def gather(shard, use, early):
    block = jnp.concatenate(
        [shard, recv(shard, "y", 1), recv(shard, "y", 2), recv(shard, "y", -1)], axis=0
    )
    half = block.shape[0] // 2
    up1, down1 = recv(block, "z", 1), recv(block, "z", -1)
    near = round_x(jnp.concatenate([block, up1, down1], axis=0), 0)
    up2, down2 = recv(up1, "z", 1), recv(down1, "z", -1)
    up3, down3 = recv(up2, "z", 1), recv(down2, "z", -1)
    last = first_of(*near[2], *early)
    far = (recv(up3[:half], "z", 1) + last, recv(down3[half:], "z", -1) + last)
    group = jnp.concatenate([up2, down2, up3, down3, *far], axis=0)
    own = use(near[0] + [group])
    rest = round_x(group, first_of(own))
    return [own] + [use(near[dx] + rest[dx]) for dx in range(1, NX)]


def place(pos, i):
    dy, dz = ORDER[i]
    at = lax.rem(pos[0] + dy, NY) * NZ + lax.rem(pos[1] + dz, NZ)
    return pl.multiple_of(at * LANES, LANES)


def norm_kernel(pos, e_ref, gain_ref, out_ref, rows):
    e = e_ref[...].astype(f32)
    scale = lax.rsqrt(jnp.mean(e * e, axis=-1, keepdims=True) + 1e-06)
    rows[...] = (e * scale * gain_ref[...].astype(f32)).astype(bf16)
    for i in range(len(ORDER)):
        out_ref[:, i * LANES : (i + 1) * LANES] = rows[:, pl.ds(place(pos, i), LANES)]


def normalise(pos, enc, gain, tile):
    rows, width = enc.shape
    block = pl.BlockSpec((tile, width), lambda i, pos: (i, 0))
    return pl.pallas_call(
        norm_kernel,
        out_shape=shaped((rows, width), bf16),
        grid_spec=pltpu.PrefetchScalarGridSpec(
            num_scalar_prefetch=1,
            grid=(rows // tile,),
            in_specs=[block, pl.BlockSpec((1, width), lambda i, pos: (0, 0))],
            out_specs=block,
            scratch_shapes=[pltpu.VMEM((tile, width), bf16)],
        ),
        compiler_params=params(12),
        cost_estimate=pl.CostEstimate(
            flops=6 * rows * width, bytes_accessed=4 * rows * width, transcendentals=0
        ),
    )(pos, enc, gain)


def project_kernel(x_ref, *refs):
    pieces, out_ref = refs[:-1], refs[-1]
    tile = min(out_ref.shape[1], 256)
    for col in range(0, out_ref.shape[1], tile):
        acc, at = None, 0
        for ref in pieces:
            depth = ref.shape[0]
            part = jnp.dot(
                x_ref[:, at : at + depth], ref[:, col : col + tile], preferred_element_type=f32
            )
            acc = part if acc is None else acc + part
            at += depth
        out_ref[:, col : col + tile] = acc.astype(bf16)


def project(x, pieces):
    rows, width = x.shape
    cols = pieces[0].shape[1]
    return pl.pallas_call(
        project_kernel,
        out_shape=shaped((rows, cols), bf16),
        in_specs=[VMEM] * (1 + len(pieces)),
        out_specs=VMEM,
        compiler_params=params(8),
        cost_estimate=pl.CostEstimate(
            flops=2 * rows * width * cols,
            bytes_accessed=2 * (rows * width + width * cols + rows * cols),
            transcendentals=0,
        ),
    )(x, *pieces)


def query_kernel(pos, dec_ref, w_ref, out_ref):
    at = pl.multiple_of((pos[0] * NZ + pos[1]) * LANES, LANES)
    part = jnp.dot(dec_ref[:, pl.ds(at, LANES)], w_ref[...], preferred_element_type=f32)
    for j in range(out_ref.shape[1]):
        out_ref[:, j, :] = part[:, j * LANES : (j + 1) * LANES]


def spread_kernel(pos, got_ref, out_ref):
    total = jnp.sum(got_ref[...], axis=0, keepdims=True)
    out_ref[...] = jnp.broadcast_to(total, out_ref.shape)


def same_head(rows, cols, answers):
    row = lax.broadcasted_iota(jnp.int32, (rows, cols), 0) // answers
    col = lax.broadcasted_iota(jnp.int32, (rows, cols), 1) // HDIM
    return row == col


def softmax_kernel(plen, pos, q_ref, *refs):
    keys, (high_ref, low_ref, stat_ref, mass_ref) = refs[:NX], refs[NX:]
    answers = q_ref.shape[0]
    lane = lax.broadcasted_iota(jnp.int32, (answers, LANES), 1)
    stats = jnp.zeros((answers, LANES), f32)
    masses = [stats] * mass_ref.shape[0]
    for dx, key_ref in enumerate(keys):
        quarter = lax.rem(pos[2] + dx, NX)
        slots, cols = key_ref.shape
        passages = slots // plen
        heads = cols // HDIM
        pairs = heads * answers
        blocks = cols // LANES
        q = jnp.concatenate(
            [q_ref[:, pl.ds(quarter * blocks + j, 1), :].reshape(answers, LANES) for j in range(blocks)],
            axis=1,
        )
        spread = jnp.where(
            same_head(pairs, cols, answers), jnp.concatenate([q] * heads, axis=0), 0.0
        ).astype(bf16)
        logits = lax.dot_general(
            spread, key_ref[...], (((1,), (1,)), ((), ())), preferred_element_type=f32
        ) * HDIM ** (-0.5)
        token = lax.broadcasted_iota(jnp.int32, (pairs, plen), 1)
        valid = [token < pos[3 + i] for i in range(passages)]
        masked = [
            jnp.where(valid[i], logits[:, i * plen : (i + 1) * plen], -1e30) for i in range(passages)
        ]
        top = functools.reduce(jnp.maximum, [jnp.max(m, axis=1, keepdims=True) for m in masked])
        p = [jnp.where(valid[i], jnp.exp(masked[i] - top), 0.0) for i in range(passages)]
        sums = [jnp.sum(part, axis=1, keepdims=True) for part in p]
        total = functools.reduce(jnp.add, sums)
        for h in range(heads):
            at = slice(h * answers, (h + 1) * answers)
            head = quarter * heads + h
            stats = jnp.where(lane == head, top[at, :], stats)
            stats = jnp.where(lane == head + LANES // 2, total[at, :], stats)
            masses = [jnp.where(lane == head, s[at, :], m) for s, m in zip(sums, masses)]
        whole = jnp.concatenate(p, axis=1)
        high = whole.astype(bf16)
        at = slice(dx * pairs, (dx + 1) * pairs)
        high_ref[at, :] = high
        low_ref[at, :] = (whole - high.astype(f32)).astype(bf16)
    stat_ref[...] = stats
    for i, mass in enumerate(masses):
        mass_ref[i] = mass


def value_kernel(pos, x_ref, high_ref, low_ref, stat_ref, v_hbm, out_ref, buf, acc, sems):
    answers, rows, _ = out_ref.shape
    pairs = high_ref.shape[0] // NX
    cols = buf.shape[1] // NX
    blocks = cols // LANES
    half = len(ORDER) // 2

    def fetch(i):
        return pltpu.make_async_copy(
            v_hbm.at[pl.ds(place(pos, i), LANES), :],
            buf.at[pl.ds(i * LANES, LANES), :],
            sems.at[i],
        )

    for i in range(len(ORDER)):
        fetch(i).start()
    for part in range(2):
        for i in range(part * half, (part + 1) * half):
            fetch(i).wait()
        at = slice(part * half * LANES, (part + 1) * half * LANES)
        for g in range(NX):
            col = slice(g * cols, (g + 1) * cols)
            v = jnp.dot(x_ref[:, at], buf[at, col], preferred_element_type=f32)
            acc[:, col] = v if part == 0 else acc[:, col] + v
    for dx in range(NX):
        quarter = lax.rem(pos[2] + dx, NX)
        v = acc[:, pl.ds(pl.multiple_of(quarter * cols, cols), cols)].astype(bf16)
        at = slice(dx * pairs, (dx + 1) * pairs)
        numer = jnp.dot(high_ref[at, :], v, preferred_element_type=f32)
        numer += jnp.dot(low_ref[at, :], v, preferred_element_type=f32)
        numer = jnp.where(same_head(pairs, cols, answers), numer, 0.0)
        total = numer[0:answers, :]
        for h in range(1, pairs // answers):
            total = total + numer[h * answers : (h + 1) * answers, :]
        for j in range(blocks):
            out_ref[:, pl.ds(quarter * blocks + j, 1), :] = total[
                :, j * LANES : (j + 1) * LANES
            ].reshape(answers, 1, LANES)
    out_ref[:, rows - 1, :] = stat_ref[...]


def by_head(lane, row, j):
    return jnp.where(lane < HDIM, row[:, 2 * j : 2 * j + 1], row[:, 2 * j + 1 : 2 * j + 2])


def merge_kernel(pos, got_ref, out_ref):
    last = got_ref.shape[1] - 1
    stats = got_ref[:, last, :]
    top = jnp.max(stats, axis=0, keepdims=True)
    scale = jnp.exp(stats - top)
    total = jnp.sum(pltpu.roll(stats, LANES // 2, 1) * scale, axis=0, keepdims=True)
    lane = lax.broadcasted_iota(jnp.int32, scale.shape, 1)
    first = lane[0:1, :]
    for j in range(last):
        numer = jnp.sum(got_ref[:, j, :] * by_head(lane, scale, j), axis=0, keepdims=True)
        row = numer / by_head(first, total, j)
        out_ref[:, j, :] = jnp.broadcast_to(row, scale.shape)
    row = jnp.where(first < LANES // 2, top, pltpu.roll(total, LANES // 2, 1))
    out_ref[:, last, :] = jnp.broadcast_to(row, scale.shape)


def out_kernel(pos, ctx_ref, stat_ref, mass_ref, w_ref, out_ref):
    answers, rows, _ = ctx_ref.shape
    last = rows - 1
    ctx = jnp.concatenate([ctx_ref[:, j, :] for j in range(last)], axis=1).astype(bf16)
    out_ref[0:answers, :] = jnp.dot(ctx, w_ref[...], preferred_element_type=f32)
    merged = ctx_ref[:, last, :]
    lane = lax.broadcasted_iota(jnp.int32, merged.shape, 1)
    heads = last * LANES // HDIM
    total = jnp.where(lane < heads, pltpu.roll(merged, LANES // 2, 1), 1.0)
    gap = jnp.where(lane < heads, stat_ref[...] - merged, 0.0)
    factor = jnp.exp(gap) / total
    first = lax.broadcasted_iota(jnp.int32, (8, LANES), 1)
    scores = jnp.zeros((8, LANES), f32)
    for i in range(mass_ref.shape[0]):
        scores = jnp.where(first == i, jnp.sum(mass_ref[i] * factor, keepdims=True), scores)
    out_ref[answers : answers + 8, :] = scores


def last_kernel(scale, pos, own_ref, other_ref, out_ref, scores_ref):
    both = own_ref[...] + other_ref[...]
    answers = out_ref.shape[0]
    out_ref[...] = both[:answers].astype(bf16)
    scores_ref[...] = both[answers : answers + 1, : scores_ref.shape[1]] * scale


def body(enc_states, lengths, enc_gain, dec_states, w_query, w_key, w_value, w_out):
    qdev, pdev, plen, width = enc_states.shape
    answers = dec_states.shape[1]
    columns = w_key.shape[1]
    pairs = columns // HDIM * answers
    slots = pdev * plen
    quarter = columns // NX
    blocks = columns // LANES
    members = NY * NZ
    x, y, z = (lax.axis_index(axis).astype(jnp.int32) for axis in ("dp", "y", "z"))
    pos = jnp.concatenate([jnp.stack([y, z, x]), lengths.reshape(pdev)])

    w_values = lax.all_gather(w_value, PSG, axis=0, tiled=True)
    normed = normalise(
        pos, enc_states.reshape(slots, width), enc_gain[None], min(slots, 128)
    )
    q_parts = call(
        query_kernel,
        shaped((answers, blocks, LANES)),
        [],
        pos,
        dec_states.reshape(answers, width),
        w_query,
    )
    q_sum = call(spread_kernel, shaped(q_parts.shape), [], pos, exchange(q_parts))
    queries = exchange(q_sum)

    mine = lax.dynamic_slice(w_key, (0, x * quarter), (w_key.shape[0], quarter))
    keys = gather(mine, functools.partial(project, normed), [q_sum])
    high, low, stat, mass = call(
        functools.partial(softmax_kernel, plen),
        [
            shaped((pairs, slots), bf16),
            shaped((pairs, slots), bf16),
            shaped((answers, LANES)),
            shaped((pdev, answers, LANES)),
        ],
        [],
        pos,
        queries,
        *keys,
        flops=2 * pairs * slots * quarter,
    )
    parts = call(
        value_kernel,
        shaped((answers, blocks + 1, LANES)),
        [
            pltpu.VMEM((width, columns), bf16),
            pltpu.VMEM((slots, columns), f32),
            pltpu.SemaphoreType.DMA((len(ORDER),)),
        ],
        pos,
        normed,
        high,
        low,
        stat,
        w_values,
        mib=46,
        flops=2 * slots * width * columns,
        hbm=(5,),
    )
    merged = call(merge_kernel, shaped(parts.shape), [], pos, exchange(parts))
    part = call(
        out_kernel,
        shaped((answers + 8, w_out.shape[1])),
        [],
        pos,
        exchange(merged),
        stat,
        mass,
        w_out,
    )
    other = lax.ppermute(part, "tp", [(0, 1), (1, 0)])
    attended, scores = call(
        functools.partial(last_kernel, pdev * members / (HEADS * answers)),
        [shaped((answers, w_out.shape[1]), bf16), shaped((1, pdev))],
        [],
        pos,
        part,
        other,
    )
    return attended[None], scores


def solution(mesh):
    fine = Mesh(mesh.devices.reshape(NX, NY, NZ, 2), ("dp", "y", "z", "tp"))
    placed = (
        P("dp", PSG, None, None),
        P("dp", PSG),
        P(),
        P("dp", None, None),
        P(PSG, "tp"),
        P(PSG, "tp"),
        P(PSG, "tp"),
        P("tp", PSG),
    )
    return jax.shard_map(
        body,
        mesh=fine,
        in_specs=placed,
        out_specs=(P("dp", None, PSG), P("dp", PSG)),
        check_vma=False,
    )
```

```python
import functools

import jax
import jax.numpy as jnp
from jax import lax
from jax.experimental import pallas as pl
from jax.experimental.pallas import tpu as pltpu
from jax.sharding import Mesh, PartitionSpec as P

HEADS = 32
HDIM = 64
NX = 4
NY = 4
NZ = 8
LANES = 128
PSG = ("y", "z")
SIZES = {"dp": NX, "y": NY, "z": NZ}
VMEM = pl.BlockSpec(memory_space=pltpu.VMEM)
SMEM = pl.BlockSpec(memory_space=pltpu.SMEM)
HBM = pl.BlockSpec(memory_space=pltpu.HBM)
f32 = jnp.float32
bf16 = jnp.bfloat16

GROUPS = ((0, 1, 7), (2, 6, 3, 5, 4))
ORDER = [(dy, dz) for group in GROUPS for dz in group for dy in range(NY)]


def shaped(shape, dtype=f32):
    return jax.ShapeDtypeStruct(shape, dtype)


def params(mib):
    return pltpu.CompilerParams(vmem_limit_bytes=mib * 1024 * 1024)


def call(kernel, outs, scratch, *args, mib=8, flops=0, hbm=()):
    specs = [SMEM] + [HBM if i in hbm else VMEM for i in range(1, len(args))]
    return pl.pallas_call(
        kernel,
        out_shape=outs,
        in_specs=specs,
        out_specs=jax.tree.map(lambda _: VMEM, outs),
        scratch_shapes=scratch,
        compiler_params=params(mib),
        cost_estimate=pl.CostEstimate(flops=flops, bytes_accessed=1 << 20, transcendentals=0),
    )(*args)


def recv(a, axis, k):
    n = SIZES[axis]
    return lax.ppermute(a, axis, [((i + k) % n, i) for i in range(n)])


def exchange(a):
    return lax.all_to_all(a, PSG, split_axis=0, concat_axis=0, tiled=True)


def pack_kernel(cuts, *refs):
    out_ref, at = refs[-1], 0
    for ref, (start, rows) in zip(refs, cuts):
        out_ref[at : at + rows, :] = ref[start : start + rows, :]
        at += rows


def pack(pieces, after=()):
    cuts = [(start, rows) for _, start, rows in pieces]
    first = pieces[0][0]
    return pl.pallas_call(
        functools.partial(pack_kernel, cuts),
        out_shape=shaped((sum(rows for _, rows in cuts), first.shape[1]), first.dtype),
        in_specs=[VMEM] * len(pieces) + [pl.BlockSpec(memory_space=pl.ANY)] * len(after),
        out_specs=VMEM,
        compiler_params=params(4),
        cost_estimate=pl.CostEstimate(flops=0, bytes_accessed=1 << 20, transcendentals=0),
    )(*[array for array, _, _ in pieces], *after)


def join(pieces, after=()):
    return pack([(piece, 0, piece.shape[0]) for piece in pieces], after)


def far_x(up, down, after=()):
    half = up.shape[0] // 2
    return [
        recv(pack([(up, 0, half)], after), "dp", 1),
        recv(pack([(down, half, half)], after), "dp", -1),
    ]


def gather(shard, use, q_sum, queries):
    block = join([shard, recv(shard, "y", 1), recv(shard, "y", 2), recv(shard, "y", -1)])
    half = block.shape[0] // 2
    up1, down1 = recv(block, "z", 1), recv(block, "z", -1)
    near = join([block, up1, down1], [q_sum])
    near_up, near_down = recv(near, "dp", 1), recv(near, "dp", -1)
    up2, down2 = recv(up1, "z", 1), recv(down1, "z", -1)
    up3, down3 = recv(up2, "z", 1), recv(down2, "z", -1)
    near_far = far_x(near_up, near_down)
    far = [
        recv(pack([(up3, 0, half)]), "z", 1),
        recv(pack([(down3, half, half)]), "z", -1),
    ]
    rest = join([up2, down2, up3, down3, *far], [queries, *near_far])
    rest_up, rest_down = recv(rest, "dp", 1), recv(rest, "dp", -1)
    (own,) = use([[near, rest]])
    rest_far = far_x(rest_up, rest_down, [own])
    key_up, key_down = use([[near_up, rest_up], [near_down, rest_down]])
    (key_far,) = use([near_far + rest_far])
    return [own, key_up, key_far, key_down]


def place(pos, i):
    dy, dz = ORDER[i]
    at = lax.rem(pos[0] + dy, NY) * NZ + lax.rem(pos[1] + dz, NZ)
    return pl.multiple_of(at * LANES, LANES)


def norm_kernel(pos, e_ref, gain_ref, out_ref, rows):
    e = e_ref[...].astype(f32)
    scale = lax.rsqrt(jnp.mean(e * e, axis=-1, keepdims=True) + 1e-06)
    rows[...] = (e * scale * gain_ref[...].astype(f32)).astype(bf16)
    for i in range(len(ORDER)):
        out_ref[:, i * LANES : (i + 1) * LANES] = rows[:, pl.ds(place(pos, i), LANES)]


def normalise(pos, enc, gain, tile):
    rows, width = enc.shape
    block = pl.BlockSpec((tile, width), lambda i, pos: (i, 0))
    return pl.pallas_call(
        norm_kernel,
        out_shape=shaped((rows, width), bf16),
        grid_spec=pltpu.PrefetchScalarGridSpec(
            num_scalar_prefetch=1,
            grid=(rows // tile,),
            in_specs=[block, pl.BlockSpec((1, width), lambda i, pos: (0, 0))],
            out_specs=block,
            scratch_shapes=[pltpu.VMEM((tile, width), bf16)],
        ),
        compiler_params=params(12),
        cost_estimate=pl.CostEstimate(
            flops=6 * rows * width, bytes_accessed=4 * rows * width, transcendentals=0
        ),
    )(pos, enc, gain)


def project_kernel(counts, x_ref, *refs):
    at_piece = 0
    for count, out_ref in zip(counts, refs[sum(counts) :]):
        acc, at = None, 0
        for ref in refs[at_piece : at_piece + count]:
            depth = ref.shape[0]
            part = jnp.dot(x_ref[:, at : at + depth], ref[...], preferred_element_type=f32)
            acc = part if acc is None else acc + part
            at += depth
        out_ref[...] = acc.astype(bf16)
        at_piece += count


def project(x, lists):
    rows, width = x.shape
    cols = lists[0][0].shape[1]
    pieces = [piece for pieces in lists for piece in pieces]
    return pl.pallas_call(
        functools.partial(project_kernel, [len(pieces) for pieces in lists]),
        out_shape=[shaped((rows, cols), bf16)] * len(lists),
        in_specs=[VMEM] * (1 + len(pieces)),
        out_specs=[VMEM] * len(lists),
        compiler_params=params(8),
        cost_estimate=pl.CostEstimate(
            flops=2 * rows * width * cols * len(lists),
            bytes_accessed=2 * (rows * width + width * cols + rows * cols),
            transcendentals=0,
        ),
    )(x, *pieces)


def query_kernel(pos, dec_ref, w_ref, out_ref):
    at = pl.multiple_of((pos[0] * NZ + pos[1]) * LANES, LANES)
    part = jnp.dot(dec_ref[:, pl.ds(at, LANES)], w_ref[...], preferred_element_type=f32)
    for j in range(out_ref.shape[1]):
        out_ref[:, j, :] = part[:, j * LANES : (j + 1) * LANES]


def spread_kernel(pos, got_ref, out_ref):
    total = jnp.sum(got_ref[...], axis=0, keepdims=True)
    out_ref[...] = jnp.broadcast_to(total, out_ref.shape)


def same_head(rows, cols, answers):
    row = lax.broadcasted_iota(jnp.int32, (rows, cols), 0) // answers
    col = lax.broadcasted_iota(jnp.int32, (rows, cols), 1) // HDIM
    return row == col


def softmax_kernel(plen, pos, q_ref, *refs):
    keys, (high_ref, low_ref, stat_ref) = refs[:NX], refs[NX:]
    answers = q_ref.shape[0]
    lane = lax.broadcasted_iota(jnp.int32, (answers, LANES), 1)
    stats = jnp.zeros((answers, LANES), f32)
    heads_all = q_ref.shape[1] * LANES // HDIM
    for dx, key_ref in enumerate(keys):
        quarter = lax.rem(pos[2] + dx, NX)
        slots, cols = key_ref.shape
        passages = slots // plen
        heads = cols // HDIM
        pairs = heads * answers
        blocks = cols // LANES
        q = jnp.concatenate(
            [q_ref[:, pl.ds(quarter * blocks + j, 1), :].reshape(answers, LANES) for j in range(blocks)],
            axis=1,
        )
        spread = jnp.where(
            same_head(pairs, cols, answers), jnp.concatenate([q] * heads, axis=0), 0.0
        ).astype(bf16)
        logits = lax.dot_general(
            spread, key_ref[...], (((1,), (1,)), ((), ())), preferred_element_type=f32
        ) * HDIM ** (-0.5)
        token = lax.broadcasted_iota(jnp.int32, (pairs, plen), 1)
        valid = [token < pos[3 + i] for i in range(passages)]
        masked = [
            jnp.where(valid[i], logits[:, i * plen : (i + 1) * plen], -1e30) for i in range(passages)
        ]
        top = functools.reduce(jnp.maximum, [jnp.max(m, axis=1, keepdims=True) for m in masked])
        p = [jnp.where(valid[i], jnp.exp(masked[i] - top), 0.0) for i in range(passages)]
        sums = [jnp.sum(part, axis=1, keepdims=True) for part in p]
        total = functools.reduce(jnp.add, sums)
        for h in range(heads):
            at = slice(h * answers, (h + 1) * answers)
            head = quarter * heads + h
            stats = jnp.where(lane == head, top[at, :], stats)
            stats = jnp.where(lane == head + LANES // 2, total[at, :], stats)
            for i, part in enumerate(sums):
                stats = jnp.where(lane == head + (i + 1) * heads_all, part[at, :], stats)
        whole = jnp.concatenate(p, axis=1)
        high = whole.astype(bf16)
        at = slice(dx * pairs, (dx + 1) * pairs)
        high_ref[at, :] = high
        low_ref[at, :] = (whole - high.astype(f32)).astype(bf16)
    stat_ref[...] = stats


def value_kernel(pos, x_hbm, high_ref, low_ref, stat_ref, v_hbm, out_ref, x_buf, buf, acc, x_sems, sems):
    answers, rows, _ = out_ref.shape
    pairs = high_ref.shape[0] // NX
    cols = buf.shape[1] // NX
    blocks = cols // LANES
    half = len(ORDER) // 2

    def fetch(i):
        return pltpu.make_async_copy(
            v_hbm.at[pl.ds(place(pos, i), LANES), :],
            buf.at[pl.ds(i * LANES, LANES), :],
            sems.at[i],
        )

    def fetch_x(part):
        at = pl.ds(part * half * LANES, half * LANES)
        return pltpu.make_async_copy(x_hbm.at[:, at], x_buf.at[:, at], x_sems.at[part])

    for part in range(2):
        fetch_x(part).start()
        for i in range(part * half, (part + 1) * half):
            fetch(i).start()
    for part in range(2):
        fetch_x(part).wait()
        for i in range(part * half, (part + 1) * half):
            fetch(i).wait()
        at = slice(part * half * LANES, (part + 1) * half * LANES)
        for g in range(NX):
            col = slice(g * cols, (g + 1) * cols)
            v = jnp.dot(x_buf[:, at], buf[at, col], preferred_element_type=f32)
            acc[:, col] = v if part == 0 else acc[:, col] + v
    for dx in range(NX):
        quarter = lax.rem(pos[2] + dx, NX)
        v = acc[:, pl.ds(pl.multiple_of(quarter * cols, cols), cols)].astype(bf16)
        at = slice(dx * pairs, (dx + 1) * pairs)
        numer = jnp.dot(high_ref[at, :], v, preferred_element_type=f32)
        numer += jnp.dot(low_ref[at, :], v, preferred_element_type=f32)
        numer = jnp.where(same_head(pairs, cols, answers), numer, 0.0)
        total = numer[0:answers, :]
        for h in range(1, pairs // answers):
            total = total + numer[h * answers : (h + 1) * answers, :]
        for j in range(blocks):
            out_ref[:, pl.ds(quarter * blocks + j, 1), :] = total[
                :, j * LANES : (j + 1) * LANES
            ].reshape(answers, 1, LANES)
    out_ref[:, rows - 1, :] = stat_ref[...]


def by_head(lane, row, j):
    return jnp.where(lane < HDIM, row[:, 2 * j : 2 * j + 1], row[:, 2 * j + 1 : 2 * j + 2])


def merge_kernel(passages, pos, got_ref, out_ref, rows):
    last = got_ref.shape[1] - 1
    heads = last * LANES // HDIM
    stats = got_ref[:, last, :]
    top = jnp.max(stats, axis=0, keepdims=True)
    scale = jnp.exp(stats - top)
    total = jnp.sum(pltpu.roll(stats, LANES // 2, 1) * scale, axis=0, keepdims=True)
    lane = lax.broadcasted_iota(jnp.int32, scale.shape, 1)
    first = lane[0:1, :]
    rows[...] = jnp.zeros_like(rows)
    for j in range(last):
        numer = jnp.sum(got_ref[:, j, :] * by_head(lane, scale, j), axis=0, keepdims=True)
        row = numer / by_head(first, total, j)
        rows[:, j, :] = jnp.broadcast_to(row, scale.shape)
    factor = jnp.where(lane < heads, scale / jnp.where(first < heads, total, 1.0), 0.0)
    parts = jnp.zeros_like(scale)
    for i in range(passages):
        own = pltpu.roll(stats, LANES - (i + 1) * heads, 1) * factor
        rest = jnp.sum(own, axis=1, keepdims=True)
        for term in range(3):
            piece = rest.astype(bf16).astype(f32)
            parts = jnp.where(lane == term * 8 + i, piece, parts)
            rest = rest - piece
    rows[:, last, :] = parts
    out_ref[...] = rows[...].astype(bf16)


def out_kernel(pos, ctx_ref, w_ref, out_ref, rows):
    answers = ctx_ref.shape[0]
    last = w_ref.shape[0] // LANES
    rows[...] = ctx_ref[...].astype(f32)
    ctx = jnp.concatenate([rows[:, j, :] for j in range(last)], axis=1).astype(bf16)
    out_ref[0:answers, :] = jnp.dot(ctx, w_ref[...], preferred_element_type=f32)
    parts = rows[:, last, :]
    scores = parts + pltpu.roll(parts, LANES - 8, 1) + pltpu.roll(parts, LANES - 16, 1)
    out_ref[answers : answers + 8, :] = jnp.broadcast_to(
        jnp.sum(scores, axis=0, keepdims=True), (8, LANES)
    )


def last_kernel(scale, pos, own_ref, other_ref, out_ref, scores_ref):
    both = own_ref[...] + other_ref[...]
    answers = out_ref.shape[0]
    out_ref[...] = both[:answers].astype(bf16)
    scores_ref[...] = both[answers : answers + 1, : scores_ref.shape[1]] * scale


def body(enc_states, lengths, enc_gain, dec_states, w_query, w_key, w_value, w_out):
    qdev, pdev, plen, width = enc_states.shape
    answers = dec_states.shape[1]
    columns = w_key.shape[1]
    pairs = columns // HDIM * answers
    slots = pdev * plen
    quarter = columns // NX
    blocks = columns // LANES
    members = NY * NZ
    x, y, z = (lax.axis_index(axis).astype(jnp.int32) for axis in ("dp", "y", "z"))
    pos = jnp.concatenate([jnp.stack([y, z, x]), lengths.reshape(pdev)])

    w_values = lax.all_gather(w_value, PSG, axis=0, tiled=True)
    normed = normalise(
        pos, enc_states.reshape(slots, width), enc_gain[None], min(slots, 128)
    )
    q_parts = call(
        query_kernel,
        shaped((answers, blocks, LANES)),
        [],
        pos,
        dec_states.reshape(answers, width),
        w_query,
    )
    q_sum = call(spread_kernel, shaped(q_parts.shape), [], pos, exchange(q_parts))
    queries = exchange(q_sum)

    mine = lax.dynamic_slice(w_key, (0, x * quarter), (w_key.shape[0], quarter))
    keys = gather(mine, functools.partial(project, normed), q_sum, queries)
    high, low, stat = call(
        functools.partial(softmax_kernel, plen),
        [
            shaped((pairs, slots), bf16),
            shaped((pairs, slots), bf16),
            shaped((answers, LANES)),
        ],
        [],
        pos,
        queries,
        *keys,
        flops=2 * pairs * slots * quarter,
    )
    parts = call(
        value_kernel,
        shaped((answers, blocks + 1, LANES)),
        [
            pltpu.VMEM((slots, width), bf16),
            pltpu.VMEM((width, columns), bf16),
            pltpu.VMEM((slots, columns), f32),
            pltpu.SemaphoreType.DMA((2,)),
            pltpu.SemaphoreType.DMA((len(ORDER),)),
        ],
        pos,
        normed,
        high,
        low,
        stat,
        w_values,
        mib=52,
        flops=2 * slots * width * columns,
        hbm=(1, 5),
    )
    rows = 2 * blocks
    merged = call(
        functools.partial(merge_kernel, pdev),
        shaped((members, rows, LANES), bf16),
        [pltpu.VMEM((members, rows, LANES), f32)],
        pos,
        exchange(parts),
    )
    part = call(
        out_kernel,
        shaped((answers + 8, w_out.shape[1])),
        [pltpu.VMEM((answers, rows, LANES), f32)],
        pos,
        exchange(merged),
        w_out,
    )
    other = lax.ppermute(part, "tp", [(0, 1), (1, 0)])
    attended, scores = call(
        functools.partial(last_kernel, pdev * members / (HEADS * answers)),
        [shaped((answers, w_out.shape[1]), bf16), shaped((1, pdev))],
        [],
        pos,
        part,
        other,
    )
    return attended[None], scores


def solution(mesh):
    fine = Mesh(mesh.devices.reshape(NX, NY, NZ, 2), ("dp", "y", "z", "tp"))
    placed = (
        P("dp", PSG, None, None),
        P("dp", PSG),
        P(),
        P("dp", None, None),
        P(PSG, "tp"),
        P(PSG, "tp"),
        P(PSG, "tp"),
        P("tp", PSG),
    )
    return jax.shard_map(
        body,
        mesh=fine,
        in_specs=placed,
        out_specs=(P("dp", None, PSG), P("dp", PSG)),
        check_vma=False,
    )
```

```python
import functools

import jax
import jax.numpy as jnp
from jax import lax
from jax.experimental import pallas as pl
from jax.experimental.pallas import tpu as pltpu
from jax.sharding import Mesh, PartitionSpec as P

HEADS = 32
HDIM = 64
NX = 4
NY = 4
NZ = 8
LANES = 128
PSG = ("y", "z")
SIZES = {"dp": NX, "y": NY, "z": NZ}
VMEM = pl.BlockSpec(memory_space=pltpu.VMEM)
SMEM = pl.BlockSpec(memory_space=pltpu.SMEM)
ANY = pl.BlockSpec(memory_space=pl.ANY)
f32 = jnp.float32
bf16 = jnp.bfloat16

GROUPS = ((0, 1, 7), (2, 6, 3, 5, 4))
ORDER = [(dy, dz) for group in GROUPS for dz in group for dy in range(NY)]


def shaped(shape, dtype=f32):
    return jax.ShapeDtypeStruct(shape, dtype)


def params(mib):
    return pltpu.CompilerParams(vmem_limit_bytes=mib * 1024 * 1024)


def call(kernel, outs, scratch, *args, mib=8, flops=0, hbm=()):
    specs = [SMEM] + [ANY if i in hbm else VMEM for i in range(1, len(args))]
    return pl.pallas_call(
        kernel,
        out_shape=outs,
        in_specs=specs,
        out_specs=jax.tree.map(lambda _: VMEM, outs),
        scratch_shapes=scratch,
        compiler_params=params(mib),
        cost_estimate=pl.CostEstimate(flops=flops, bytes_accessed=1 << 20, transcendentals=0),
    )(*args)


def recv(a, axis, k):
    n = SIZES[axis]
    return lax.ppermute(a, axis, [((i + k) % n, i) for i in range(n)])


def exchange(a):
    return lax.all_to_all(a, PSG, split_axis=0, concat_axis=0, tiled=True)


def pack_kernel(cuts, *refs):
    out_ref, at = refs[-1], 0
    for ref, (start, rows) in zip(refs, cuts):
        out_ref[at : at + rows, :] = ref[start : start + rows, :]
        at += rows


def pack(pieces, after=()):
    cuts = [(start, rows) for _, start, rows in pieces]
    first = pieces[0][0]
    return pl.pallas_call(
        functools.partial(pack_kernel, cuts),
        out_shape=shaped((sum(rows for _, rows in cuts), first.shape[1]), first.dtype),
        in_specs=[VMEM] * len(pieces) + [ANY] * len(after),
        out_specs=VMEM,
        compiler_params=params(4),
        cost_estimate=pl.CostEstimate(flops=0, bytes_accessed=1 << 20, transcendentals=0),
    )(*[array for array, _, _ in pieces], *after)


def join(pieces, after=()):
    return pack([(piece, 0, piece.shape[0]) for piece in pieces], after)


def far_x(up, down, after=()):
    half = up.shape[0] // 2
    return [
        recv(pack([(up, 0, half)], after), "dp", 1),
        recv(pack([(down, half, half)], after), "dp", -1),
    ]


def gather(shard, use, late):
    block = join([shard, recv(shard, "y", 1), recv(shard, "y", 2), recv(shard, "y", -1)])
    half = block.shape[0] // 2
    up1, down1 = recv(block, "z", 1), recv(block, "z", -1)
    near = join([block, up1, down1])
    near_up, near_down = recv(near, "dp", 1), recv(near, "dp", -1)
    up2, down2 = recv(up1, "z", 1), recv(down1, "z", -1)
    up3, down3 = recv(up2, "z", 1), recv(down2, "z", -1)
    near_far = far_x(near_up, near_down)
    far = [
        recv(pack([(up3, 0, half)]), "z", 1),
        recv(pack([(down3, half, half)]), "z", -1),
    ]
    rest = join([up2, down2, up3, down3, *far], near_far)
    rest_up, rest_down = recv(rest, "dp", 1), recv(rest, "dp", -1)
    (own,) = use([[near, rest]])
    rest_far = far_x(rest_up, rest_down, [own])
    key_up, key_down = use([[near_up, rest_up], [near_down, rest_down]], late)
    (key_far,) = use([near_far + rest_far])
    return [own, key_up, key_far, key_down]


def place(pos, i):
    dy, dz = ORDER[i]
    at = lax.rem(pos[0] + dy, NY) * NZ + lax.rem(pos[1] + dz, NZ)
    return pl.multiple_of(at * LANES, LANES)


def norm_kernel(pos, e_ref, gain_ref, after_ref, out_ref, rows):
    e = e_ref[...].astype(f32)
    scale = lax.rsqrt(jnp.mean(e * e, axis=-1, keepdims=True) + 1e-06)
    rows[...] = (e * scale * gain_ref[...].astype(f32)).astype(bf16)
    for i in range(len(ORDER)):
        out_ref[:, i * LANES : (i + 1) * LANES] = rows[:, pl.ds(place(pos, i), LANES)]


def normalise(pos, enc, gain, after, tile):
    rows, width = enc.shape
    block = pl.BlockSpec((tile, width), lambda i, pos: (i, 0))
    return pl.pallas_call(
        norm_kernel,
        out_shape=shaped((rows, width), bf16),
        grid_spec=pltpu.PrefetchScalarGridSpec(
            num_scalar_prefetch=1,
            grid=(rows // tile,),
            in_specs=[
                block,
                pl.BlockSpec((1, width), lambda i, pos: (0, 0)),
                ANY,
            ],
            out_specs=block,
            scratch_shapes=[pltpu.VMEM((tile, width), bf16)],
        ),
        compiler_params=params(44),
        cost_estimate=pl.CostEstimate(
            flops=6 * rows * width, bytes_accessed=4 * rows * width, transcendentals=0
        ),
    )(pos, enc, gain, after)


def project_kernel(counts, x_ref, *refs):
    at_piece = 0
    for count, out_ref in zip(counts, refs[len(refs) - len(counts) :]):
        acc, at = None, 0
        for ref in refs[at_piece : at_piece + count]:
            depth = ref.shape[0]
            part = jnp.dot(x_ref[:, at : at + depth], ref[...], preferred_element_type=f32)
            acc = part if acc is None else acc + part
            at += depth
        out_ref[...] = acc.astype(bf16)
        at_piece += count


def project(x, lists, after=()):
    rows, width = x.shape
    cols = lists[0][0].shape[1]
    pieces = [piece for pieces in lists for piece in pieces]
    return pl.pallas_call(
        functools.partial(project_kernel, [len(pieces) for pieces in lists]),
        out_shape=[shaped((rows, cols), bf16)] * len(lists),
        in_specs=[VMEM] * (1 + len(pieces)) + [ANY] * len(after),
        out_specs=[VMEM] * len(lists),
        compiler_params=params(8),
        cost_estimate=pl.CostEstimate(
            flops=2 * rows * width * cols * len(lists),
            bytes_accessed=2 * (rows * width + width * cols + rows * cols),
            transcendentals=0,
        ),
    )(x, *pieces, *after)


def query_kernel(pos, dec_ref, w_ref, after_ref, out_ref):
    at = pl.multiple_of((pos[0] * NZ + pos[1]) * LANES, LANES)
    part = jnp.dot(dec_ref[:, pl.ds(at, LANES)], w_ref[...], preferred_element_type=f32)
    for j in range(out_ref.shape[1]):
        out_ref[:, j, :] = part[:, j * LANES : (j + 1) * LANES]


def spread_kernel(pos, got_ref, out_ref):
    total = jnp.sum(got_ref[...], axis=0, keepdims=True)
    out_ref[...] = jnp.broadcast_to(total, out_ref.shape)


def same_head(rows, cols, answers):
    row = lax.broadcasted_iota(jnp.int32, (rows, cols), 0) // answers
    col = lax.broadcasted_iota(jnp.int32, (rows, cols), 1) // HDIM
    return row == col


def softmax(plen, pos, q_ref, keys, high_ref, low_ref, stat_ref):
    answers = q_ref.shape[0]
    lane = lax.broadcasted_iota(jnp.int32, (answers, LANES), 1)
    stats = jnp.zeros((answers, LANES), f32)
    heads_all = q_ref.shape[1] * LANES // HDIM
    for dx, key_ref in enumerate(keys):
        quarter = lax.rem(pos[2] + dx, NX)
        slots, cols = key_ref.shape
        passages = slots // plen
        heads = cols // HDIM
        pairs = heads * answers
        blocks = cols // LANES
        q = jnp.concatenate(
            [q_ref[:, pl.ds(quarter * blocks + j, 1), :].reshape(answers, LANES) for j in range(blocks)],
            axis=1,
        )
        spread = jnp.where(
            same_head(pairs, cols, answers), jnp.concatenate([q] * heads, axis=0), 0.0
        ).astype(bf16)
        logits = lax.dot_general(
            spread, key_ref[...], (((1,), (1,)), ((), ())), preferred_element_type=f32
        ) * HDIM ** (-0.5)
        token = lax.broadcasted_iota(jnp.int32, (pairs, plen), 1)
        valid = [token < pos[3 + i] for i in range(passages)]
        masked = [
            jnp.where(valid[i], logits[:, i * plen : (i + 1) * plen], -1e30) for i in range(passages)
        ]
        top = functools.reduce(jnp.maximum, [jnp.max(m, axis=1, keepdims=True) for m in masked])
        p = [jnp.where(valid[i], jnp.exp(masked[i] - top), 0.0) for i in range(passages)]
        sums = [jnp.sum(part, axis=1, keepdims=True) for part in p]
        total = functools.reduce(jnp.add, sums)
        for h in range(heads):
            at = slice(h * answers, (h + 1) * answers)
            head = quarter * heads + h
            stats = jnp.where(lane == head, top[at, :], stats)
            stats = jnp.where(lane == head + LANES // 2, total[at, :], stats)
            for i, part in enumerate(sums):
                stats = jnp.where(lane == head + (i + 1) * heads_all, part[at, :], stats)
        whole = jnp.concatenate(p, axis=1)
        high = whole.astype(bf16)
        at = slice(dx * pairs, (dx + 1) * pairs)
        high_ref[at, :] = high
        low_ref[at, :] = (whole - high.astype(f32)).astype(bf16)
    stat_ref[...] = stats


def attend_kernel(plen, pos, q_ref, *refs):
    keys, refs = refs[:NX], refs[NX:]
    x_hbm, v_hbm, out_ref, high_ref, low_ref, stat_ref, x_buf, buf, acc, x_sems, sems = refs
    answers, rows, _ = out_ref.shape
    pairs = high_ref.shape[0] // NX
    cols = buf.shape[1] // NX
    blocks = cols // LANES
    half = len(ORDER) // 2

    def fetch(i):
        return pltpu.make_async_copy(
            v_hbm.at[pl.ds(place(pos, i), LANES), :],
            buf.at[pl.ds(i * LANES, LANES), :],
            sems.at[i],
        )

    def fetch_x(part):
        at = pl.ds(part * half * LANES, half * LANES)
        return pltpu.make_async_copy(x_hbm.at[:, at], x_buf.at[:, at], x_sems.at[part])

    for part in range(2):
        fetch_x(part).start()
        for i in range(part * half, (part + 1) * half):
            fetch(i).start()
    softmax(plen, pos, q_ref, keys, high_ref, low_ref, stat_ref)
    for part in range(2):
        fetch_x(part).wait()
        for i in range(part * half, (part + 1) * half):
            fetch(i).wait()
        at = slice(part * half * LANES, (part + 1) * half * LANES)
        for g in range(NX):
            col = slice(g * cols, (g + 1) * cols)
            v = jnp.dot(x_buf[:, at], buf[at, col], preferred_element_type=f32)
            acc[:, col] = v if part == 0 else acc[:, col] + v
    for dx in range(NX):
        quarter = lax.rem(pos[2] + dx, NX)
        v = acc[:, pl.ds(pl.multiple_of(quarter * cols, cols), cols)].astype(bf16)
        at = slice(dx * pairs, (dx + 1) * pairs)
        numer = jnp.dot(high_ref[at, :], v, preferred_element_type=f32)
        numer += jnp.dot(low_ref[at, :], v, preferred_element_type=f32)
        numer = jnp.where(same_head(pairs, cols, answers), numer, 0.0)
        total = numer[0:answers, :]
        for h in range(1, pairs // answers):
            total = total + numer[h * answers : (h + 1) * answers, :]
        for j in range(blocks):
            out_ref[:, pl.ds(quarter * blocks + j, 1), :] = total[
                :, j * LANES : (j + 1) * LANES
            ].reshape(answers, 1, LANES)
    out_ref[:, rows - 1, :] = stat_ref[...]


def by_head(lane, row, j):
    return jnp.where(lane < HDIM, row[:, 2 * j : 2 * j + 1], row[:, 2 * j + 1 : 2 * j + 2])


def merge_kernel(passages, pos, got_ref, out_ref, rows):
    last = got_ref.shape[1] - 1
    heads = last * LANES // HDIM
    stats = got_ref[:, last, :]
    top = jnp.max(stats, axis=0, keepdims=True)
    scale = jnp.exp(stats - top)
    total = jnp.sum(pltpu.roll(stats, LANES // 2, 1) * scale, axis=0, keepdims=True)
    lane = lax.broadcasted_iota(jnp.int32, scale.shape, 1)
    first = lane[0:1, :]
    rows[...] = jnp.zeros_like(rows)
    for j in range(last):
        numer = jnp.sum(got_ref[:, j, :] * by_head(lane, scale, j), axis=0, keepdims=True)
        row = numer / by_head(first, total, j)
        rows[:, j, :] = jnp.broadcast_to(row, scale.shape)
    factor = jnp.where(lane < heads, scale / jnp.where(first < heads, total, 1.0), 0.0)
    parts = jnp.zeros_like(scale)
    for i in range(passages):
        own = pltpu.roll(stats, LANES - (i + 1) * heads, 1) * factor
        rest = jnp.sum(own, axis=1, keepdims=True)
        for term in range(3):
            piece = rest.astype(bf16).astype(f32)
            parts = jnp.where(lane == term * 8 + i, piece, parts)
            rest = rest - piece
    rows[:, last, :] = parts
    out_ref[...] = rows[...].astype(bf16)


def out_kernel(pos, ctx_ref, w_ref, out_ref, rows):
    answers = ctx_ref.shape[0]
    last = w_ref.shape[0] // LANES
    rows[...] = ctx_ref[...].astype(f32)
    ctx = jnp.concatenate([rows[:, j, :] for j in range(last)], axis=1).astype(bf16)
    out_ref[0:answers, :] = jnp.dot(ctx, w_ref[...], preferred_element_type=f32)
    parts = rows[:, last, :]
    scores = parts + pltpu.roll(parts, LANES - 8, 1) + pltpu.roll(parts, LANES - 16, 1)
    out_ref[answers : answers + 8, :] = jnp.broadcast_to(
        jnp.sum(scores, axis=0, keepdims=True), (8, LANES)
    )


def last_kernel(scale, pos, own_ref, other_ref, out_ref, scores_ref):
    both = own_ref[...] + other_ref[...]
    answers = out_ref.shape[0]
    out_ref[...] = both[:answers].astype(bf16)
    scores_ref[...] = both[answers : answers + 1, : scores_ref.shape[1]] * scale


def body(enc_states, lengths, enc_gain, dec_states, w_query, w_key, w_value, w_out):
    qdev, pdev, plen, width = enc_states.shape
    answers = dec_states.shape[1]
    columns = w_key.shape[1]
    pairs = columns // HDIM * answers
    slots = pdev * plen
    quarter = columns // NX
    blocks = columns // LANES
    members = NY * NZ
    x, y, z = (lax.axis_index(axis).astype(jnp.int32) for axis in ("dp", "y", "z"))
    pos = jnp.concatenate([jnp.stack([y, z, x]), lengths.reshape(pdev)])

    w_values = lax.all_gather(w_value, PSG, axis=0, tiled=True)
    gain = enc_gain[None]
    q_parts = call(
        query_kernel,
        shaped((answers, blocks, LANES)),
        [],
        pos,
        dec_states.reshape(answers, width),
        w_query,
        gain,
        hbm=(3,),
    )
    q_sum = call(spread_kernel, shaped(q_parts.shape), [], pos, exchange(q_parts))
    queries = exchange(q_sum)
    normed = normalise(
        pos, enc_states.reshape(slots, width), gain, q_sum, min(slots, 128)
    )

    mine = lax.dynamic_slice(w_key, (0, x * quarter), (w_key.shape[0], quarter))
    keys = gather(mine, functools.partial(project, normed), [queries])
    parts = call(
        functools.partial(attend_kernel, plen),
        shaped((answers, blocks + 1, LANES)),
        [
            pltpu.VMEM((pairs, slots), bf16),
            pltpu.VMEM((pairs, slots), bf16),
            pltpu.VMEM((answers, LANES), f32),
            pltpu.VMEM((slots, width), bf16),
            pltpu.VMEM((width, columns), bf16),
            pltpu.VMEM((slots, columns), f32),
            pltpu.SemaphoreType.DMA((2,)),
            pltpu.SemaphoreType.DMA((len(ORDER),)),
        ],
        pos,
        queries,
        *keys,
        normed,
        w_values,
        mib=52,
        flops=2 * slots * width * columns,
        hbm=(2 + NX, 3 + NX),
    )
    rows = 2 * blocks
    merged = call(
        functools.partial(merge_kernel, pdev),
        shaped((members, rows, LANES), bf16),
        [pltpu.VMEM((members, rows, LANES), f32)],
        pos,
        exchange(parts),
    )
    part = call(
        out_kernel,
        shaped((answers + 8, w_out.shape[1])),
        [pltpu.VMEM((answers, rows, LANES), f32)],
        pos,
        exchange(merged),
        w_out,
    )
    other = lax.ppermute(part, "tp", [(0, 1), (1, 0)])
    attended, scores = call(
        functools.partial(last_kernel, pdev * members / (HEADS * answers)),
        [shaped((answers, w_out.shape[1]), bf16), shaped((1, pdev))],
        [],
        pos,
        part,
        other,
    )
    return attended[None], scores


def solution(mesh):
    fine = Mesh(mesh.devices.reshape(NX, NY, NZ, 2), ("dp", "y", "z", "tp"))
    placed = (
        P("dp", PSG, None, None),
        P("dp", PSG),
        P(),
        P("dp", None, None),
        P(PSG, "tp"),
        P(PSG, "tp"),
        P(PSG, "tp"),
        P("tp", PSG),
    )
    return jax.shard_map(
        body,
        mesh=fine,
        in_specs=placed,
        out_specs=(P("dp", None, PSG), P("dp", PSG)),
        check_vma=False,
    )
```

```python
import functools

import jax
import jax.numpy as jnp
from jax import lax
from jax.experimental import pallas as pl
from jax.experimental.pallas import tpu as pltpu
from jax.sharding import Mesh, PartitionSpec as P

HEADS = 32
HDIM = 64
NX = 4
NY = 4
NZ = 8
LANES = 128
PSG = ("y", "z")
SIZES = {"dp": NX, "y": NY, "z": NZ}
VMEM = pl.BlockSpec(memory_space=pltpu.VMEM)
SMEM = pl.BlockSpec(memory_space=pltpu.SMEM)
ANY = pl.BlockSpec(memory_space=pl.ANY)
f32 = jnp.float32
bf16 = jnp.bfloat16

GROUPS = ((0, 1, 7), (2, 6, 3, 5, 4))
ORDER = [(dy, dz) for group in GROUPS for dz in group for dy in range(NY)]


def shaped(shape, dtype=f32):
    return jax.ShapeDtypeStruct(shape, dtype)


def params(mib):
    return pltpu.CompilerParams(vmem_limit_bytes=mib * 1024 * 1024)


def call(kernel, outs, scratch, *args, mib=8, flops=0, hbm=()):
    specs = [SMEM] + [ANY if i in hbm else VMEM for i in range(1, len(args))]
    return pl.pallas_call(
        kernel,
        out_shape=outs,
        in_specs=specs,
        out_specs=jax.tree.map(lambda _: VMEM, outs),
        scratch_shapes=scratch,
        compiler_params=params(mib),
        cost_estimate=pl.CostEstimate(flops=flops, bytes_accessed=1 << 20, transcendentals=0),
    )(*args)


def recv(a, axis, k):
    n = SIZES[axis]
    return lax.ppermute(a, axis, [((i + k) % n, i) for i in range(n)])


def exchange(a):
    return lax.all_to_all(a, PSG, split_axis=0, concat_axis=0, tiled=True)


def pack_kernel(cuts, *refs):
    out_ref, at = refs[-1], 0
    for ref, (start, rows) in zip(refs, cuts):
        out_ref[at : at + rows, :] = ref[start : start + rows, :]
        at += rows


def pack(pieces, after=()):
    cuts = [(start, rows) for _, start, rows in pieces]
    first = pieces[0][0]
    return pl.pallas_call(
        functools.partial(pack_kernel, cuts),
        out_shape=shaped((sum(rows for _, rows in cuts), first.shape[1]), first.dtype),
        in_specs=[VMEM] * len(pieces) + [ANY] * len(after),
        out_specs=VMEM,
        compiler_params=params(4),
        cost_estimate=pl.CostEstimate(flops=0, bytes_accessed=1 << 20, transcendentals=0),
    )(*[array for array, _, _ in pieces], *after)


def join(pieces, after=()):
    return pack([(piece, 0, piece.shape[0]) for piece in pieces], after)


def far_x(up, down, after=()):
    half = up.shape[0] // 2
    return [
        recv(pack([(up, 0, half)], after), "dp", 1),
        recv(pack([(down, half, half)], after), "dp", -1),
    ]


def gather(shard, use, first, second, third):
    block = join([shard, recv(shard, "y", 1), recv(shard, "y", 2), recv(shard, "y", -1)])
    half = block.shape[0] // 2
    up1, down1 = recv(block, "z", 1), recv(block, "z", -1)
    near = join([block, up1, down1], [first])
    near_up, near_down = recv(near, "dp", 1), recv(near, "dp", -1)
    up2, down2 = recv(up1, "z", 1), recv(down1, "z", -1)
    up3, down3 = recv(up2, "z", 1), recv(down2, "z", -1)
    near_far = far_x(near_up, near_down)
    far = [
        recv(pack([(up3, 0, half)]), "z", 1),
        recv(pack([(down3, half, half)]), "z", -1),
    ]
    rest = join([up2, down2, up3, down3, *far], near_far)
    rest_up, rest_down = recv(rest, "dp", 1), recv(rest, "dp", -1)
    (own,) = use([[near, rest]], [second])
    rest_far = far_x(rest_up, rest_down, [own])
    (key_up,) = use([[near_up, rest_up]], [third])
    (key_down,) = use([[near_down, rest_down]], [third])
    (key_far,) = use([near_far + rest_far])
    return [own, key_up, key_far, key_down]


def place(pos, i):
    dy, dz = ORDER[i]
    at = lax.rem(pos[0] + dy, NY) * NZ + lax.rem(pos[1] + dz, NZ)
    return pl.multiple_of(at * LANES, LANES)


def norm_kernel(pos, e_ref, gain_ref, out_ref, rows):
    e = e_ref[...].astype(f32)
    scale = lax.rsqrt(jnp.mean(e * e, axis=-1, keepdims=True) + 1e-06)
    rows[...] = (e * scale * gain_ref[...].astype(f32)).astype(bf16)
    for i in range(len(ORDER)):
        out_ref[:, i * LANES : (i + 1) * LANES] = rows[:, pl.ds(place(pos, i), LANES)]


def normalise(pos, enc, gain, tile):
    rows, width = enc.shape
    block = pl.BlockSpec((tile, width), lambda i, pos: (i, 0))
    return pl.pallas_call(
        norm_kernel,
        out_shape=shaped((rows, width), bf16),
        grid_spec=pltpu.PrefetchScalarGridSpec(
            num_scalar_prefetch=1,
            grid=(rows // tile,),
            in_specs=[
                block,
                pl.BlockSpec((1, width), lambda i, pos: (0, 0)),
            ],
            out_specs=block,
            scratch_shapes=[pltpu.VMEM((tile, width), bf16)],
        ),
        compiler_params=params(44),
        cost_estimate=pl.CostEstimate(
            flops=6 * rows * width, bytes_accessed=4 * rows * width, transcendentals=0
        ),
    )(pos, enc, gain)


def project_kernel(counts, x_ref, *refs):
    at_piece = 0
    for count, out_ref in zip(counts, refs[len(refs) - len(counts) :]):
        acc, at = None, 0
        for ref in refs[at_piece : at_piece + count]:
            depth = ref.shape[0]
            part = jnp.dot(x_ref[:, at : at + depth], ref[...], preferred_element_type=f32)
            acc = part if acc is None else acc + part
            at += depth
        out_ref[...] = acc.astype(bf16)
        at_piece += count


def project(x, lists, after=()):
    rows, width = x.shape
    cols = lists[0][0].shape[1]
    pieces = [piece for pieces in lists for piece in pieces]
    return pl.pallas_call(
        functools.partial(project_kernel, [len(pieces) for pieces in lists]),
        out_shape=[shaped((rows, cols), bf16)] * len(lists),
        in_specs=[VMEM] * (1 + len(pieces)) + [ANY] * len(after),
        out_specs=[VMEM] * len(lists),
        compiler_params=params(8),
        cost_estimate=pl.CostEstimate(
            flops=2 * rows * width * cols * len(lists),
            bytes_accessed=2 * (rows * width + width * cols + rows * cols),
            transcendentals=0,
        ),
    )(x, *pieces, *after)


def query_kernel(pos, dec_ref, w_ref, after_ref, out_ref):
    at = pl.multiple_of((pos[0] * NZ + pos[1]) * LANES, LANES)
    part = jnp.dot(dec_ref[:, pl.ds(at, LANES)], w_ref[...], preferred_element_type=f32)
    for j in range(out_ref.shape[1]):
        out_ref[:, j, :] = part[:, j * LANES : (j + 1) * LANES]


def spread_kernel(pos, got_ref, out_ref):
    total = jnp.sum(got_ref[...], axis=0, keepdims=True)
    out_ref[...] = jnp.broadcast_to(total, out_ref.shape)


def same_head(rows, cols, answers):
    row = lax.broadcasted_iota(jnp.int32, (rows, cols), 0) // answers
    col = lax.broadcasted_iota(jnp.int32, (rows, cols), 1) // HDIM
    return row == col


def softmax(plen, pos, q_ref, keys, high_ref, low_ref, stat_ref):
    answers = q_ref.shape[0]
    lane = lax.broadcasted_iota(jnp.int32, (answers, LANES), 1)
    stats = jnp.zeros((answers, LANES), f32)
    heads_all = q_ref.shape[1] * LANES // HDIM
    for dx, key_ref in enumerate(keys):
        quarter = lax.rem(pos[2] + dx, NX)
        slots, cols = key_ref.shape
        passages = slots // plen
        heads = cols // HDIM
        pairs = heads * answers
        blocks = cols // LANES
        q = jnp.concatenate(
            [q_ref[:, pl.ds(quarter * blocks + j, 1), :].reshape(answers, LANES) for j in range(blocks)],
            axis=1,
        )
        spread = jnp.where(
            same_head(pairs, cols, answers), jnp.concatenate([q] * heads, axis=0), 0.0
        ).astype(bf16)
        logits = lax.dot_general(
            spread, key_ref[...], (((1,), (1,)), ((), ())), preferred_element_type=f32
        ) * HDIM ** (-0.5)
        token = lax.broadcasted_iota(jnp.int32, (pairs, plen), 1)
        valid = [token < pos[3 + i] for i in range(passages)]
        masked = [
            jnp.where(valid[i], logits[:, i * plen : (i + 1) * plen], -1e30) for i in range(passages)
        ]
        top = functools.reduce(jnp.maximum, [jnp.max(m, axis=1, keepdims=True) for m in masked])
        p = [jnp.where(valid[i], jnp.exp(masked[i] - top), 0.0) for i in range(passages)]
        sums = [jnp.sum(part, axis=1, keepdims=True) for part in p]
        total = functools.reduce(jnp.add, sums)
        for h in range(heads):
            at = slice(h * answers, (h + 1) * answers)
            head = quarter * heads + h
            stats = jnp.where(lane == head, top[at, :], stats)
            stats = jnp.where(lane == head + LANES // 2, total[at, :], stats)
            for i, part in enumerate(sums):
                stats = jnp.where(lane == head + (i + 1) * heads_all, part[at, :], stats)
        whole = jnp.concatenate(p, axis=1)
        high = whole.astype(bf16)
        at = slice(dx * pairs, (dx + 1) * pairs)
        high_ref[at, :] = high
        low_ref[at, :] = (whole - high.astype(f32)).astype(bf16)
    stat_ref[...] = stats


def attend_kernel(plen, pos, q_ref, *refs):
    keys, refs = refs[:NX], refs[NX:]
    x_hbm, v_hbm, out_ref, k_buf, high_ref, low_ref, stat_ref, x_buf, buf, acc, k_sems, x_sems, sems = refs
    answers, rows, _ = out_ref.shape
    pairs = high_ref.shape[0] // NX
    cols = buf.shape[1] // NX
    blocks = cols // LANES
    half = len(ORDER) // 2

    def fetch(i):
        return pltpu.make_async_copy(
            v_hbm.at[pl.ds(place(pos, i), LANES), :],
            buf.at[pl.ds(i * LANES, LANES), :],
            sems.at[i],
        )

    def fetch_x(part):
        at = pl.ds(part * half * LANES, half * LANES)
        return pltpu.make_async_copy(x_hbm.at[:, at], x_buf.at[:, at], x_sems.at[part])

    def fetch_key(i):
        return pltpu.make_async_copy(keys[i], k_buf.at[i], k_sems.at[i])

    for i in range(NX):
        fetch_key(i).start()
    for part in range(2):
        fetch_x(part).start()
        for i in range(part * half, (part + 1) * half):
            fetch(i).start()
    for i in range(NX):
        fetch_key(i).wait()
    softmax(plen, pos, q_ref, [k_buf.at[i] for i in range(NX)], high_ref, low_ref, stat_ref)
    for part in range(2):
        fetch_x(part).wait()
        for i in range(part * half, (part + 1) * half):
            fetch(i).wait()
        at = slice(part * half * LANES, (part + 1) * half * LANES)
        for g in range(NX):
            col = slice(g * cols, (g + 1) * cols)
            v = jnp.dot(x_buf[:, at], buf[at, col], preferred_element_type=f32)
            acc[:, col] = v if part == 0 else acc[:, col] + v
    for dx in range(NX):
        quarter = lax.rem(pos[2] + dx, NX)
        v = acc[:, pl.ds(pl.multiple_of(quarter * cols, cols), cols)].astype(bf16)
        at = slice(dx * pairs, (dx + 1) * pairs)
        numer = jnp.dot(high_ref[at, :], v, preferred_element_type=f32)
        numer += jnp.dot(low_ref[at, :], v, preferred_element_type=f32)
        numer = jnp.where(same_head(pairs, cols, answers), numer, 0.0)
        total = numer[0:answers, :]
        for h in range(1, pairs // answers):
            total = total + numer[h * answers : (h + 1) * answers, :]
        for j in range(blocks):
            out_ref[:, pl.ds(quarter * blocks + j, 1), :] = total[
                :, j * LANES : (j + 1) * LANES
            ].reshape(answers, 1, LANES)
    out_ref[:, rows - 1, :] = stat_ref[...]


def by_head(lane, row, j):
    return jnp.where(lane < HDIM, row[:, 2 * j : 2 * j + 1], row[:, 2 * j + 1 : 2 * j + 2])


def merge_kernel(passages, pos, got_ref, out_ref, rows):
    last = got_ref.shape[1] - 1
    heads = last * LANES // HDIM
    stats = got_ref[:, last, :]
    top = jnp.max(stats, axis=0, keepdims=True)
    scale = jnp.exp(stats - top)
    total = jnp.sum(pltpu.roll(stats, LANES // 2, 1) * scale, axis=0, keepdims=True)
    lane = lax.broadcasted_iota(jnp.int32, scale.shape, 1)
    first = lane[0:1, :]
    rows[...] = jnp.zeros_like(rows)
    for j in range(last):
        numer = jnp.sum(got_ref[:, j, :] * by_head(lane, scale, j), axis=0, keepdims=True)
        row = numer / by_head(first, total, j)
        rows[:, j, :] = jnp.broadcast_to(row, scale.shape)
    factor = jnp.where(lane < heads, scale / jnp.where(first < heads, total, 1.0), 0.0)
    parts = jnp.zeros_like(scale)
    for i in range(passages):
        own = pltpu.roll(stats, LANES - (i + 1) * heads, 1) * factor
        rest = jnp.sum(own, axis=1, keepdims=True)
        for term in range(3):
            piece = rest.astype(bf16).astype(f32)
            parts = jnp.where(lane == term * 8 + i, piece, parts)
            rest = rest - piece
    rows[:, last, :] = parts
    out_ref[...] = rows[...].astype(bf16)


def out_kernel(pos, ctx_ref, w_ref, out_ref, rows):
    answers = ctx_ref.shape[0]
    last = w_ref.shape[0] // LANES
    rows[...] = ctx_ref[...].astype(f32)
    ctx = jnp.concatenate([rows[:, j, :] for j in range(last)], axis=1).astype(bf16)
    out_ref[0:answers, :] = jnp.dot(ctx, w_ref[...], preferred_element_type=f32)
    parts = rows[:, last, :]
    scores = parts + pltpu.roll(parts, LANES - 8, 1) + pltpu.roll(parts, LANES - 16, 1)
    out_ref[answers : answers + 8, :] = jnp.broadcast_to(
        jnp.sum(scores, axis=0, keepdims=True), (8, LANES)
    )


def last_kernel(scale, pos, own_ref, other_ref, out_ref, scores_ref):
    both = own_ref[...] + other_ref[...]
    answers = out_ref.shape[0]
    out_ref[...] = both[:answers].astype(bf16)
    scores_ref[...] = both[answers : answers + 1, : scores_ref.shape[1]] * scale


def body(enc_states, lengths, enc_gain, dec_states, w_query, w_key, w_value, w_out):
    qdev, pdev, plen, width = enc_states.shape
    answers = dec_states.shape[1]
    columns = w_key.shape[1]
    pairs = columns // HDIM * answers
    slots = pdev * plen
    quarter = columns // NX
    blocks = columns // LANES
    members = NY * NZ
    x, y, z = (lax.axis_index(axis).astype(jnp.int32) for axis in ("dp", "y", "z"))
    pos = jnp.concatenate([jnp.stack([y, z, x]), lengths.reshape(pdev)])

    w_values = lax.all_gather(w_value, PSG, axis=0, tiled=True)
    gain = enc_gain[None]
    q_parts = call(
        query_kernel,
        shaped((answers, blocks, LANES)),
        [],
        pos,
        dec_states.reshape(answers, width),
        w_query,
        gain,
        hbm=(3,),
    )
    q_sum = call(spread_kernel, shaped(q_parts.shape), [], pos, exchange(q_parts))
    queries = exchange(q_sum)
    normed = normalise(
        pos, enc_states.reshape(slots, width), gain, min(slots, 128)
    )

    mine = lax.dynamic_slice(w_key, (0, x * quarter), (w_key.shape[0], quarter))
    keys = gather(mine, functools.partial(project, normed), normed, q_sum, queries)
    parts = call(
        functools.partial(attend_kernel, plen),
        shaped((answers, blocks + 1, LANES)),
        [
            pltpu.VMEM((NX, slots, quarter), bf16),
            pltpu.VMEM((pairs, slots), bf16),
            pltpu.VMEM((pairs, slots), bf16),
            pltpu.VMEM((answers, LANES), f32),
            pltpu.VMEM((slots, width), bf16),
            pltpu.VMEM((width, columns), bf16),
            pltpu.VMEM((slots, columns), f32),
            pltpu.SemaphoreType.DMA((NX,)),
            pltpu.SemaphoreType.DMA((2,)),
            pltpu.SemaphoreType.DMA((len(ORDER),)),
        ],
        pos,
        queries,
        *keys,
        normed,
        w_values,
        mib=52,
        flops=2 * slots * width * columns,
        hbm=tuple(range(2, 4 + NX)),
    )
    rows = 2 * blocks
    merged = call(
        functools.partial(merge_kernel, pdev),
        shaped((members, rows, LANES), bf16),
        [pltpu.VMEM((members, rows, LANES), f32)],
        pos,
        exchange(parts),
    )
    part = call(
        out_kernel,
        shaped((answers + 8, w_out.shape[1])),
        [pltpu.VMEM((answers, rows, LANES), f32)],
        pos,
        exchange(merged),
        w_out,
    )
    other = lax.ppermute(part, "tp", [(0, 1), (1, 0)])
    attended, scores = call(
        functools.partial(last_kernel, pdev * members / (HEADS * answers)),
        [shaped((answers, w_out.shape[1]), bf16), shaped((1, pdev))],
        [],
        pos,
        part,
        other,
    )
    return attended[None], scores


def solution(mesh):
    fine = Mesh(mesh.devices.reshape(NX, NY, NZ, 2), ("dp", "y", "z", "tp"))
    placed = (
        P("dp", PSG, None, None),
        P("dp", PSG),
        P(),
        P("dp", None, None),
        P(PSG, "tp"),
        P(PSG, "tp"),
        P(PSG, "tp"),
        P("tp", PSG),
    )
    return jax.shard_map(
        body,
        mesh=fine,
        in_specs=placed,
        out_specs=(P("dp", None, PSG), P("dp", PSG)),
        check_vma=False,
    )
```

```python
import functools

import jax
import jax.numpy as jnp
from jax import lax
from jax.experimental import pallas as pl
from jax.experimental.pallas import tpu as pltpu
from jax.sharding import Mesh, PartitionSpec as P

HEADS = 32
HDIM = 64
NX = 4
NY = 4
NZ = 8
LANES = 128
PARTS = 4
PSG = ("y", "z")
SIZES = {"dp": NX, "y": NY, "z": NZ}
VMEM = pl.BlockSpec(memory_space=pltpu.VMEM)
SMEM = pl.BlockSpec(memory_space=pltpu.SMEM)
ANY = pl.BlockSpec(memory_space=pl.ANY)
f32 = jnp.float32
bf16 = jnp.bfloat16

GROUPS = ((0, 1, 7), (2, 6, 3, 5, 4))
ORDER = [(dy, dz) for group in GROUPS for dz in group for dy in range(NY)]


def shaped(shape, dtype=f32):
    return jax.ShapeDtypeStruct(shape, dtype)


def params(mib):
    return pltpu.CompilerParams(vmem_limit_bytes=mib * 1024 * 1024)


def call(kernel, outs, scratch, *args, mib=8, flops=0, hbm=()):
    specs = [SMEM] + [ANY if i in hbm else VMEM for i in range(1, len(args))]
    return pl.pallas_call(
        kernel,
        out_shape=outs,
        in_specs=specs,
        out_specs=jax.tree.map(lambda _: VMEM, outs),
        scratch_shapes=scratch,
        compiler_params=params(mib),
        cost_estimate=pl.CostEstimate(flops=flops, bytes_accessed=1 << 20, transcendentals=0),
    )(*args)


def recv(a, axis, k):
    n = SIZES[axis]
    return lax.ppermute(a, axis, [((i + k) % n, i) for i in range(n)])


def exchange(a):
    return lax.all_to_all(a, PSG, split_axis=0, concat_axis=0, tiled=True)


def pack_kernel(cuts, *refs):
    out_ref, at = refs[-1], 0
    for ref, (start, rows) in zip(refs, cuts):
        out_ref[at : at + rows, :] = ref[start : start + rows, :]
        at += rows


def pack(pieces, after=()):
    cuts = [(start, rows) for _, start, rows in pieces]
    first = pieces[0][0]
    return pl.pallas_call(
        functools.partial(pack_kernel, cuts),
        out_shape=shaped((sum(rows for _, rows in cuts), first.shape[1]), first.dtype),
        in_specs=[VMEM] * len(pieces) + [ANY] * len(after),
        out_specs=VMEM,
        compiler_params=params(4),
        cost_estimate=pl.CostEstimate(flops=0, bytes_accessed=1 << 20, transcendentals=0),
    )(*[array for array, _, _ in pieces], *after)


def join(pieces, after=()):
    return pack([(piece, 0, piece.shape[0]) for piece in pieces], after)


def far_x(up, down, after=()):
    half = up.shape[0] // 2
    return [
        recv(pack([(up, 0, half)], after), "dp", 1),
        recv(pack([(down, half, half)], after), "dp", -1),
    ]


def gather(shard, use, first, second, third):
    block = join([shard, recv(shard, "y", 1), recv(shard, "y", 2), recv(shard, "y", -1)])
    half = block.shape[0] // 2
    up1, down1 = recv(block, "z", 1), recv(block, "z", -1)
    near = join([block, up1, down1], [first])
    near_up, near_down = recv(near, "dp", 1), recv(near, "dp", -1)
    up2, down2 = recv(up1, "z", 1), recv(down1, "z", -1)
    up3, down3 = recv(up2, "z", 1), recv(down2, "z", -1)
    near_far = far_x(near_up, near_down)
    far = [
        recv(pack([(up3, 0, half)]), "z", 1),
        recv(pack([(down3, half, half)]), "z", -1),
    ]
    rest = join([up2, down2, up3, down3, *far], near_far)
    rest_up, rest_down = recv(rest, "dp", 1), recv(rest, "dp", -1)
    (own,) = use([[near, rest]], [second])
    rest_far = far_x(rest_up, rest_down, [own])
    (key_up,) = use([[near_up, rest_up]], [third])
    (key_down,) = use([[near_down, rest_down]], [third])
    (key_far,) = use([near_far + rest_far])
    return [own, key_up, key_far, key_down]


def place(pos, i):
    dy, dz = ORDER[i]
    at = lax.rem(pos[0] + dy, NY) * NZ + lax.rem(pos[1] + dz, NZ)
    return pl.multiple_of(at * LANES, LANES)


def norm_kernel(pos, e_ref, gain_ref, out_ref, rows):
    e = e_ref[...].astype(f32)
    scale = lax.rsqrt(jnp.mean(e * e, axis=-1, keepdims=True) + 1e-06)
    rows[...] = (e * scale * gain_ref[...].astype(f32)).astype(bf16)
    for i in range(len(ORDER)):
        out_ref[:, i * LANES : (i + 1) * LANES] = rows[:, pl.ds(place(pos, i), LANES)]


def normalise(pos, enc, gain, tile):
    rows, width = enc.shape
    block = pl.BlockSpec((tile, width), lambda i, pos: (i, 0))
    return pl.pallas_call(
        norm_kernel,
        out_shape=shaped((rows, width), bf16),
        grid_spec=pltpu.PrefetchScalarGridSpec(
            num_scalar_prefetch=1,
            grid=(rows // tile,),
            in_specs=[
                block,
                pl.BlockSpec((1, width), lambda i, pos: (0, 0)),
            ],
            out_specs=block,
            scratch_shapes=[pltpu.VMEM((tile, width), bf16)],
        ),
        compiler_params=params(44),
        cost_estimate=pl.CostEstimate(
            flops=6 * rows * width, bytes_accessed=4 * rows * width, transcendentals=0
        ),
    )(pos, enc, gain)


def project_kernel(counts, x_ref, *refs):
    at_piece = 0
    for count, out_ref in zip(counts, refs[len(refs) - len(counts) :]):
        acc, at = None, 0
        for ref in refs[at_piece : at_piece + count]:
            depth = ref.shape[0]
            part = jnp.dot(x_ref[:, at : at + depth], ref[...], preferred_element_type=f32)
            acc = part if acc is None else acc + part
            at += depth
        out_ref[...] = acc.astype(bf16)
        at_piece += count


def project(x, lists, after=()):
    rows, width = x.shape
    cols = lists[0][0].shape[1]
    pieces = [piece for pieces in lists for piece in pieces]
    return pl.pallas_call(
        functools.partial(project_kernel, [len(pieces) for pieces in lists]),
        out_shape=[shaped((rows, cols), bf16)] * len(lists),
        in_specs=[VMEM] * (1 + len(pieces)) + [ANY] * len(after),
        out_specs=[VMEM] * len(lists),
        compiler_params=params(8),
        cost_estimate=pl.CostEstimate(
            flops=2 * rows * width * cols * len(lists),
            bytes_accessed=2 * (rows * width + width * cols + rows * cols),
            transcendentals=0,
        ),
    )(x, *pieces, *after)


def query_kernel(pos, dec_ref, w_ref, after_ref, out_ref):
    at = pl.multiple_of((pos[0] * NZ + pos[1]) * LANES, LANES)
    part = jnp.dot(dec_ref[:, pl.ds(at, LANES)], w_ref[...], preferred_element_type=f32)
    for j in range(out_ref.shape[1]):
        out_ref[:, j, :] = part[:, j * LANES : (j + 1) * LANES]


def spread_kernel(pos, got_ref, out_ref):
    total = jnp.sum(got_ref[...], axis=0, keepdims=True)
    out_ref[...] = jnp.broadcast_to(total, out_ref.shape)


def same_head(rows, cols, answers):
    row = lax.broadcasted_iota(jnp.int32, (rows, cols), 0) // answers
    col = lax.broadcasted_iota(jnp.int32, (rows, cols), 1) // HDIM
    return row == col


def softmax(plen, pos, q_ref, keys, high_ref, low_ref, stat_ref):
    answers = q_ref.shape[0]
    lane = lax.broadcasted_iota(jnp.int32, (answers, LANES), 1)
    stats = jnp.zeros((answers, LANES), f32)
    heads_all = q_ref.shape[1] * LANES // HDIM
    for dx, key_ref in enumerate(keys):
        quarter = lax.rem(pos[2] + dx, NX)
        slots, cols = key_ref.shape
        passages = slots // plen
        heads = cols // HDIM
        pairs = heads * answers
        blocks = cols // LANES
        q = jnp.concatenate(
            [q_ref[:, pl.ds(quarter * blocks + j, 1), :].reshape(answers, LANES) for j in range(blocks)],
            axis=1,
        )
        spread = jnp.where(
            same_head(pairs, cols, answers), jnp.concatenate([q] * heads, axis=0), 0.0
        ).astype(bf16)
        logits = lax.dot_general(
            spread, key_ref[...], (((1,), (1,)), ((), ())), preferred_element_type=f32
        ) * HDIM ** (-0.5)
        token = lax.broadcasted_iota(jnp.int32, (pairs, plen), 1)
        valid = [token < pos[3 + i] for i in range(passages)]
        masked = [
            jnp.where(valid[i], logits[:, i * plen : (i + 1) * plen], -1e30) for i in range(passages)
        ]
        top = functools.reduce(jnp.maximum, [jnp.max(m, axis=1, keepdims=True) for m in masked])
        p = [jnp.where(valid[i], jnp.exp(masked[i] - top), 0.0) for i in range(passages)]
        sums = [jnp.sum(part, axis=1, keepdims=True) for part in p]
        total = functools.reduce(jnp.add, sums)
        for h in range(heads):
            at = slice(h * answers, (h + 1) * answers)
            head = quarter * heads + h
            stats = jnp.where(lane == head, top[at, :], stats)
            stats = jnp.where(lane == head + LANES // 2, total[at, :], stats)
            for i, part in enumerate(sums):
                stats = jnp.where(lane == head + (i + 1) * heads_all, part[at, :], stats)
        whole = jnp.concatenate(p, axis=1)
        high = whole.astype(bf16)
        at = slice(dx * pairs, (dx + 1) * pairs)
        high_ref[at, :] = high
        low_ref[at, :] = (whole - high.astype(f32)).astype(bf16)
    stat_ref[...] = stats


def attend_kernel(plen, pos, q_ref, *refs):
    keys, refs = refs[:NX], refs[NX:]
    x_hbm, v_hbm, out_ref, k_buf, high_ref, low_ref, stat_ref, x_buf, buf, acc, k_sems, x_sems, sems = refs
    answers, rows, _ = out_ref.shape
    pairs = high_ref.shape[0] // NX
    cols = buf.shape[1] // NX
    blocks = cols // LANES
    per = len(ORDER) // PARTS

    def fetch(i):
        return pltpu.make_async_copy(
            v_hbm.at[pl.ds(place(pos, i), LANES), :],
            buf.at[pl.ds(i * LANES, LANES), :],
            sems.at[i],
        )

    def fetch_x(part):
        at = pl.ds(part * per * LANES, per * LANES)
        return pltpu.make_async_copy(x_hbm.at[:, at], x_buf.at[:, at], x_sems.at[part])

    def fetch_key(i):
        return pltpu.make_async_copy(keys[i], k_buf.at[i], k_sems.at[i])

    for i in range(NX):
        fetch_key(i).start()
    for part in range(PARTS):
        fetch_x(part).start()
        for i in range(part * per, (part + 1) * per):
            fetch(i).start()
    for i in range(NX):
        fetch_key(i).wait()
    softmax(plen, pos, q_ref, [k_buf.at[i] for i in range(NX)], high_ref, low_ref, stat_ref)
    for part in range(PARTS):
        fetch_x(part).wait()
        for i in range(part * per, (part + 1) * per):
            fetch(i).wait()
        at = slice(part * per * LANES, (part + 1) * per * LANES)
        for g in range(NX):
            col = slice(g * cols, (g + 1) * cols)
            v = jnp.dot(x_buf[:, at], buf[at, col], preferred_element_type=f32)
            acc[:, col] = v if part == 0 else acc[:, col] + v
    for dx in range(NX):
        quarter = lax.rem(pos[2] + dx, NX)
        v = acc[:, pl.ds(pl.multiple_of(quarter * cols, cols), cols)].astype(bf16)
        at = slice(dx * pairs, (dx + 1) * pairs)
        numer = jnp.dot(high_ref[at, :], v, preferred_element_type=f32)
        numer += jnp.dot(low_ref[at, :], v, preferred_element_type=f32)
        numer = jnp.where(same_head(pairs, cols, answers), numer, 0.0)
        total = numer[0:answers, :]
        for h in range(1, pairs // answers):
            total = total + numer[h * answers : (h + 1) * answers, :]
        for j in range(blocks):
            out_ref[:, pl.ds(quarter * blocks + j, 1), :] = total[
                :, j * LANES : (j + 1) * LANES
            ].reshape(answers, 1, LANES)
    out_ref[:, rows - 1, :] = stat_ref[...]


def by_head(lane, row, j):
    return jnp.where(lane < HDIM, row[:, 2 * j : 2 * j + 1], row[:, 2 * j + 1 : 2 * j + 2])


def merge_kernel(passages, pos, got_ref, out_ref, rows):
    last = got_ref.shape[1] - 1
    heads = last * LANES // HDIM
    stats = got_ref[:, last, :]
    top = jnp.max(stats, axis=0, keepdims=True)
    scale = jnp.exp(stats - top)
    total = jnp.sum(pltpu.roll(stats, LANES // 2, 1) * scale, axis=0, keepdims=True)
    lane = lax.broadcasted_iota(jnp.int32, scale.shape, 1)
    first = lane[0:1, :]
    rows[...] = jnp.zeros_like(rows)
    for j in range(last):
        numer = jnp.sum(got_ref[:, j, :] * by_head(lane, scale, j), axis=0, keepdims=True)
        row = numer / by_head(first, total, j)
        rows[:, j, :] = jnp.broadcast_to(row, scale.shape)
    factor = jnp.where(lane < heads, scale / jnp.where(first < heads, total, 1.0), 0.0)
    parts = jnp.zeros_like(scale)
    for i in range(passages):
        own = pltpu.roll(stats, LANES - (i + 1) * heads, 1) * factor
        rest = jnp.sum(own, axis=1, keepdims=True)
        for term in range(3):
            piece = rest.astype(bf16).astype(f32)
            parts = jnp.where(lane == term * 8 + i, piece, parts)
            rest = rest - piece
    rows[:, last, :] = parts
    out_ref[...] = rows[...].astype(bf16)


def out_kernel(pos, ctx_ref, w_ref, out_ref, rows):
    answers = ctx_ref.shape[0]
    last = w_ref.shape[0] // LANES
    rows[...] = ctx_ref[...].astype(f32)
    ctx = jnp.concatenate([rows[:, j, :] for j in range(last)], axis=1).astype(bf16)
    out_ref[0:answers, :] = jnp.dot(ctx, w_ref[...], preferred_element_type=f32)
    parts = rows[:, last, :]
    scores = parts + pltpu.roll(parts, LANES - 8, 1) + pltpu.roll(parts, LANES - 16, 1)
    out_ref[answers : answers + 8, :] = jnp.broadcast_to(
        jnp.sum(scores, axis=0, keepdims=True), (8, LANES)
    )


def last_kernel(scale, pos, own_ref, other_ref, out_ref, scores_ref):
    both = own_ref[...] + other_ref[...]
    answers = out_ref.shape[0]
    out_ref[...] = both[:answers].astype(bf16)
    scores_ref[...] = both[answers : answers + 1, : scores_ref.shape[1]] * scale


def body(enc_states, lengths, enc_gain, dec_states, w_query, w_key, w_value, w_out):
    qdev, pdev, plen, width = enc_states.shape
    answers = dec_states.shape[1]
    columns = w_key.shape[1]
    pairs = columns // HDIM * answers
    slots = pdev * plen
    quarter = columns // NX
    blocks = columns // LANES
    members = NY * NZ
    x, y, z = (lax.axis_index(axis).astype(jnp.int32) for axis in ("dp", "y", "z"))
    pos = jnp.concatenate([jnp.stack([y, z, x]), lengths.reshape(pdev)])

    w_values = lax.all_gather(w_value, PSG, axis=0, tiled=True)
    gain = enc_gain[None]
    q_parts = call(
        query_kernel,
        shaped((answers, blocks, LANES)),
        [],
        pos,
        dec_states.reshape(answers, width),
        w_query,
        gain,
        hbm=(3,),
    )
    q_sum = call(spread_kernel, shaped(q_parts.shape), [], pos, exchange(q_parts))
    queries = exchange(q_sum)
    normed = normalise(
        pos, enc_states.reshape(slots, width), gain, min(slots, 128)
    )

    mine = lax.dynamic_slice(w_key, (0, x * quarter), (w_key.shape[0], quarter))
    keys = gather(mine, functools.partial(project, normed), normed, q_sum, queries)
    parts = call(
        functools.partial(attend_kernel, plen),
        shaped((answers, blocks + 1, LANES)),
        [
            pltpu.VMEM((NX, slots, quarter), bf16),
            pltpu.VMEM((pairs, slots), bf16),
            pltpu.VMEM((pairs, slots), bf16),
            pltpu.VMEM((answers, LANES), f32),
            pltpu.VMEM((slots, width), bf16),
            pltpu.VMEM((width, columns), bf16),
            pltpu.VMEM((slots, columns), f32),
            pltpu.SemaphoreType.DMA((NX,)),
            pltpu.SemaphoreType.DMA((PARTS,)),
            pltpu.SemaphoreType.DMA((len(ORDER),)),
        ],
        pos,
        queries,
        *keys,
        normed,
        w_values,
        mib=52,
        flops=2 * slots * width * columns,
        hbm=tuple(range(2, 4 + NX)),
    )
    rows = 2 * blocks
    merged = call(
        functools.partial(merge_kernel, pdev),
        shaped((members, rows, LANES), bf16),
        [pltpu.VMEM((members, rows, LANES), f32)],
        pos,
        exchange(parts),
    )
    part = call(
        out_kernel,
        shaped((answers + 8, w_out.shape[1])),
        [pltpu.VMEM((answers, rows, LANES), f32)],
        pos,
        exchange(merged),
        w_out,
    )
    other = lax.ppermute(part, "tp", [(0, 1), (1, 0)])
    attended, scores = call(
        functools.partial(last_kernel, pdev * members / (HEADS * answers)),
        [shaped((answers, w_out.shape[1]), bf16), shaped((1, pdev))],
        [],
        pos,
        part,
        other,
    )
    return attended[None], scores


def solution(mesh):
    fine = Mesh(mesh.devices.reshape(NX, NY, NZ, 2), ("dp", "y", "z", "tp"))
    placed = (
        P("dp", PSG, None, None),
        P("dp", PSG),
        P(),
        P("dp", None, None),
        P(PSG, "tp"),
        P(PSG, "tp"),
        P(PSG, "tp"),
        P("tp", PSG),
    )
    return jax.shard_map(
        body,
        mesh=fine,
        in_specs=placed,
        out_specs=(P("dp", None, PSG), P("dp", PSG)),
        check_vma=False,
    )
```

```python
import functools

import jax
import jax.numpy as jnp
from jax import lax
from jax.experimental import pallas as pl
from jax.experimental.pallas import tpu as pltpu
from jax.sharding import Mesh, PartitionSpec as P

HEADS = 32
HDIM = 64
NX = 4
NY = 4
NZ = 8
LANES = 128
PARTS = 4
PSG = ("y", "z")
SIZES = {"dp": NX, "y": NY, "z": NZ}
VMEM = pl.BlockSpec(memory_space=pltpu.VMEM)
SMEM = pl.BlockSpec(memory_space=pltpu.SMEM)
ANY = pl.BlockSpec(memory_space=pl.ANY)
f32 = jnp.float32
bf16 = jnp.bfloat16

GROUPS = ((0, 1, 7), (2, 6, 3, 5, 4))
ORDER = [(dy, dz) for group in GROUPS for dz in group for dy in range(NY)]


def shaped(shape, dtype=f32):
    return jax.ShapeDtypeStruct(shape, dtype)


def params(mib):
    return pltpu.CompilerParams(vmem_limit_bytes=mib * 1024 * 1024)


def call(kernel, outs, scratch, *args, mib=8, flops=0, hbm=()):
    specs = [SMEM] + [ANY if i in hbm else VMEM for i in range(1, len(args))]
    return pl.pallas_call(
        kernel,
        out_shape=outs,
        in_specs=specs,
        out_specs=jax.tree.map(lambda _: VMEM, outs),
        scratch_shapes=scratch,
        compiler_params=params(mib),
        cost_estimate=pl.CostEstimate(flops=flops, bytes_accessed=1 << 20, transcendentals=0),
    )(*args)


def recv(a, axis, k):
    n = SIZES[axis]
    return lax.ppermute(a, axis, [((i + k) % n, i) for i in range(n)])


def exchange(a):
    return lax.all_to_all(a, PSG, split_axis=0, concat_axis=0, tiled=True)


def pack_kernel(cuts, *refs):
    out_ref, at = refs[-1], 0
    for ref, (start, rows) in zip(refs, cuts):
        out_ref[at : at + rows, :] = ref[start : start + rows, :]
        at += rows


def pack(pieces, after=()):
    cuts = [(start, rows) for _, start, rows in pieces]
    first = pieces[0][0]
    return pl.pallas_call(
        functools.partial(pack_kernel, cuts),
        out_shape=shaped((sum(rows for _, rows in cuts), first.shape[1]), first.dtype),
        in_specs=[VMEM] * len(pieces) + [ANY] * len(after),
        out_specs=VMEM,
        compiler_params=params(4),
        cost_estimate=pl.CostEstimate(flops=0, bytes_accessed=1 << 20, transcendentals=0),
    )(*[array for array, _, _ in pieces], *after)


def join(pieces, after=()):
    return pack([(piece, 0, piece.shape[0]) for piece in pieces], after)


def far_x(up, down, after=()):
    half = up.shape[0] // 2
    return [
        recv(pack([(up, 0, half)], after), "dp", 1),
        recv(pack([(down, half, half)], after), "dp", -1),
    ]


def gather(shard, use, first, second, third):
    block = join([shard, recv(shard, "y", 1), recv(shard, "y", 2), recv(shard, "y", -1)])
    half = block.shape[0] // 2
    up1, down1 = recv(block, "z", 1), recv(block, "z", -1)
    near = join([block, up1, down1], [first])
    near_up, near_down = recv(near, "dp", 1), recv(near, "dp", -1)
    up2, down2 = recv(up1, "z", 1), recv(down1, "z", -1)
    up3, down3 = recv(up2, "z", 1), recv(down2, "z", -1)
    near_far = far_x(near_up, near_down)
    far = [
        recv(pack([(up3, 0, half)]), "z", 1),
        recv(pack([(down3, half, half)]), "z", -1),
    ]
    rest = join([up2, down2, up3, down3, *far], near_far)
    rest_up, rest_down = recv(rest, "dp", 1), recv(rest, "dp", -1)
    (own,) = use([[near, rest]], [second])
    rest_far = far_x(rest_up, rest_down, [own])
    (key_up,) = use([[near_up, rest_up]], [third])
    (key_down,) = use([[near_down, rest_down]], [third])
    (key_far,) = use([near_far + rest_far])
    return [own, key_up, key_far, key_down]


def place(pos, i):
    dy, dz = ORDER[i]
    at = lax.rem(pos[0] + dy, NY) * NZ + lax.rem(pos[1] + dz, NZ)
    return pl.multiple_of(at * LANES, LANES)


def norm_kernel(pos, e_ref, gain_ref, out_ref, rows):
    e = e_ref[...].astype(f32)
    scale = lax.rsqrt(jnp.mean(e * e, axis=-1, keepdims=True) + 1e-06)
    rows[...] = (e * scale * gain_ref[...].astype(f32)).astype(bf16)
    for i in range(len(ORDER)):
        out_ref[:, i * LANES : (i + 1) * LANES] = rows[:, pl.ds(place(pos, i), LANES)]


def normalise(pos, enc, gain, tile):
    rows, width = enc.shape
    block = pl.BlockSpec((tile, width), lambda i, pos: (i, 0))
    return pl.pallas_call(
        norm_kernel,
        out_shape=shaped((rows, width), bf16),
        grid_spec=pltpu.PrefetchScalarGridSpec(
            num_scalar_prefetch=1,
            grid=(rows // tile,),
            in_specs=[
                block,
                pl.BlockSpec((1, width), lambda i, pos: (0, 0)),
            ],
            out_specs=block,
            scratch_shapes=[pltpu.VMEM((tile, width), bf16)],
        ),
        compiler_params=params(44),
        cost_estimate=pl.CostEstimate(
            flops=6 * rows * width, bytes_accessed=4 * rows * width, transcendentals=0
        ),
    )(pos, enc, gain)


def project_kernel(counts, x_ref, *refs):
    at_piece = 0
    for count, out_ref in zip(counts, refs[len(refs) - len(counts) :]):
        acc, at = None, 0
        for ref in refs[at_piece : at_piece + count]:
            depth = ref.shape[0]
            part = jnp.dot(x_ref[:, at : at + depth], ref[...], preferred_element_type=f32)
            acc = part if acc is None else acc + part
            at += depth
        out_ref[...] = acc.astype(bf16)
        at_piece += count


def project(x, lists, after=()):
    rows, width = x.shape
    cols = lists[0][0].shape[1]
    pieces = [piece for pieces in lists for piece in pieces]
    return pl.pallas_call(
        functools.partial(project_kernel, [len(pieces) for pieces in lists]),
        out_shape=[shaped((rows, cols), bf16)] * len(lists),
        in_specs=[VMEM] * (1 + len(pieces)) + [ANY] * len(after),
        out_specs=[VMEM] * len(lists),
        compiler_params=params(8),
        cost_estimate=pl.CostEstimate(
            flops=2 * rows * width * cols * len(lists),
            bytes_accessed=2 * (rows * width + width * cols + rows * cols),
            transcendentals=0,
        ),
    )(x, *pieces, *after)


def query_kernel(pos, dec_ref, w_ref, after_ref, out_ref):
    at = pl.multiple_of((pos[0] * NZ + pos[1]) * LANES, LANES)
    part = jnp.dot(dec_ref[:, pl.ds(at, LANES)], w_ref[...], preferred_element_type=f32)
    for j in range(out_ref.shape[1]):
        out_ref[:, j, :] = part[:, j * LANES : (j + 1) * LANES]


def spread_kernel(pos, got_ref, out_ref):
    total = jnp.sum(got_ref[...], axis=0, keepdims=True)
    out_ref[...] = jnp.broadcast_to(total, out_ref.shape)


def same_head(rows, cols, answers):
    row = lax.broadcasted_iota(jnp.int32, (rows, cols), 0) // answers
    col = lax.broadcasted_iota(jnp.int32, (rows, cols), 1) // HDIM
    return row == col


def softmax(plen, pos, q_ref, keys, high_ref, low_ref, stat_ref):
    answers = q_ref.shape[0]
    lane = lax.broadcasted_iota(jnp.int32, (answers, LANES), 1)
    stats = jnp.zeros((answers, LANES), f32)
    heads_all = q_ref.shape[1] * LANES // HDIM
    for dx, key_ref in enumerate(keys):
        quarter = lax.rem(pos[2] + dx, NX)
        slots, cols = key_ref.shape
        passages = slots // plen
        heads = cols // HDIM
        pairs = heads * answers
        blocks = cols // LANES
        q = jnp.concatenate(
            [q_ref[:, pl.ds(quarter * blocks + j, 1), :].reshape(answers, LANES) for j in range(blocks)],
            axis=1,
        )
        spread = jnp.where(
            same_head(pairs, cols, answers), jnp.concatenate([q] * heads, axis=0), 0.0
        ).astype(bf16)
        logits = lax.dot_general(
            spread, key_ref[...], (((1,), (1,)), ((), ())), preferred_element_type=f32
        ) * HDIM ** (-0.5)
        token = lax.broadcasted_iota(jnp.int32, (pairs, plen), 1)
        valid = [token < pos[3 + i] for i in range(passages)]
        masked = [
            jnp.where(valid[i], logits[:, i * plen : (i + 1) * plen], -1e30) for i in range(passages)
        ]
        top = functools.reduce(jnp.maximum, [jnp.max(m, axis=1, keepdims=True) for m in masked])
        p = [jnp.where(valid[i], jnp.exp(masked[i] - top), 0.0) for i in range(passages)]
        sums = [jnp.sum(part, axis=1, keepdims=True) for part in p]
        total = functools.reduce(jnp.add, sums)
        for h in range(heads):
            at = slice(h * answers, (h + 1) * answers)
            head = quarter * heads + h
            stats = jnp.where(lane == head, top[at, :], stats)
            stats = jnp.where(lane == head + LANES // 2, total[at, :], stats)
            for i, part in enumerate(sums):
                stats = jnp.where(lane == head + (i + 1) * heads_all, part[at, :], stats)
        whole = jnp.concatenate(p, axis=1)
        high = whole.astype(bf16)
        at = slice(dx * pairs, (dx + 1) * pairs)
        high_ref[at, :] = high
        low_ref[at, :] = (whole - high.astype(f32)).astype(bf16)
    stat_ref[...] = stats


def attend_kernel(plen, pos, q_ref, *refs):
    keys, refs = refs[:NX], refs[NX:]
    x_hbm, v_hbm, out_ref, k_buf, high_ref, low_ref, stat_ref, x_buf, buf, acc, k_sems, x_sems, sems = refs
    answers, rows, _ = out_ref.shape
    pairs = high_ref.shape[0] // NX
    cols = buf.shape[1] // NX
    blocks = cols // LANES
    per = len(ORDER) // PARTS

    def fetch(i):
        return pltpu.make_async_copy(
            v_hbm.at[pl.ds(place(pos, i), LANES), :],
            buf.at[pl.ds(i * LANES, LANES), :],
            sems.at[i],
        )

    def fetch_x(part):
        at = pl.ds(part * per * LANES, per * LANES)
        return pltpu.make_async_copy(x_hbm.at[:, at], x_buf.at[:, at], x_sems.at[part])

    def fetch_key(i):
        return pltpu.make_async_copy(keys[i], k_buf.at[i], k_sems.at[i])

    for i in range(NX):
        fetch_key(i).start()
    for part in range(PARTS):
        fetch_x(part).start()
        for i in range(part * per, (part + 1) * per):
            fetch(i).start()
    for i in range(NX):
        fetch_key(i).wait()
    softmax(plen, pos, q_ref, [k_buf.at[i] for i in range(NX)], high_ref, low_ref, stat_ref)
    for part in range(PARTS):
        fetch_x(part).wait()
        for i in range(part * per, (part + 1) * per):
            fetch(i).wait()
        at = slice(part * per * LANES, (part + 1) * per * LANES)
        for g in range(NX):
            col = slice(g * cols, (g + 1) * cols)
            v = jnp.dot(x_buf[:, at], buf[at, col], preferred_element_type=f32)
            acc[:, col] = v if part == 0 else acc[:, col] + v
    for dx in range(NX):
        quarter = lax.rem(pos[2] + dx, NX)
        v = acc[:, pl.ds(pl.multiple_of(quarter * cols, cols), cols)].astype(bf16)
        at = slice(dx * pairs, (dx + 1) * pairs)
        both = jnp.concatenate([high_ref[at, :], low_ref[at, :]], axis=0)
        sums = jnp.dot(both, v, preferred_element_type=f32)
        numer = sums[:pairs, :] + sums[pairs:, :]
        numer = jnp.where(same_head(pairs, cols, answers), numer, 0.0)
        total = numer[0:answers, :]
        for h in range(1, pairs // answers):
            total = total + numer[h * answers : (h + 1) * answers, :]
        for j in range(blocks):
            out_ref[:, pl.ds(quarter * blocks + j, 1), :] = total[
                :, j * LANES : (j + 1) * LANES
            ].reshape(answers, 1, LANES)
    out_ref[:, rows - 1, :] = stat_ref[...]


def by_head(lane, row, j):
    return jnp.where(lane < HDIM, row[:, 2 * j : 2 * j + 1], row[:, 2 * j + 1 : 2 * j + 2])


def merge_kernel(passages, pos, got_ref, out_ref, rows):
    last = got_ref.shape[1] - 1
    heads = last * LANES // HDIM
    stats = got_ref[:, last, :]
    top = jnp.max(stats, axis=0, keepdims=True)
    scale = jnp.exp(stats - top)
    total = jnp.sum(pltpu.roll(stats, LANES // 2, 1) * scale, axis=0, keepdims=True)
    lane = lax.broadcasted_iota(jnp.int32, scale.shape, 1)
    first = lane[0:1, :]
    rows[...] = jnp.zeros_like(rows)
    for j in range(last):
        numer = jnp.sum(got_ref[:, j, :] * by_head(lane, scale, j), axis=0, keepdims=True)
        row = numer / by_head(first, total, j)
        rows[:, j, :] = jnp.broadcast_to(row, scale.shape)
    factor = jnp.where(lane < heads, scale / jnp.where(first < heads, total, 1.0), 0.0)
    parts = jnp.zeros_like(scale)
    for i in range(passages):
        own = pltpu.roll(stats, LANES - (i + 1) * heads, 1) * factor
        rest = jnp.sum(own, axis=1, keepdims=True)
        for term in range(3):
            piece = rest.astype(bf16).astype(f32)
            parts = jnp.where(lane == term * 8 + i, piece, parts)
            rest = rest - piece
    rows[:, last, :] = parts
    out_ref[...] = rows[...].astype(bf16)


def out_kernel(pos, ctx_ref, w_ref, out_ref, rows):
    answers = ctx_ref.shape[0]
    last = w_ref.shape[0] // LANES
    rows[...] = ctx_ref[...].astype(f32)
    ctx = jnp.concatenate([rows[:, j, :] for j in range(last)], axis=1).astype(bf16)
    out_ref[0:answers, :] = jnp.dot(ctx, w_ref[...], preferred_element_type=f32)
    parts = rows[:, last, :]
    scores = parts + pltpu.roll(parts, LANES - 8, 1) + pltpu.roll(parts, LANES - 16, 1)
    out_ref[answers : answers + 8, :] = jnp.broadcast_to(
        jnp.sum(scores, axis=0, keepdims=True), (8, LANES)
    )


def last_kernel(scale, pos, own_ref, other_ref, out_ref, scores_ref):
    both = own_ref[...] + other_ref[...]
    answers = out_ref.shape[0]
    out_ref[...] = both[:answers].astype(bf16)
    scores_ref[...] = both[answers : answers + 1, : scores_ref.shape[1]] * scale


def body(enc_states, lengths, enc_gain, dec_states, w_query, w_key, w_value, w_out):
    qdev, pdev, plen, width = enc_states.shape
    answers = dec_states.shape[1]
    columns = w_key.shape[1]
    pairs = columns // HDIM * answers
    slots = pdev * plen
    quarter = columns // NX
    blocks = columns // LANES
    members = NY * NZ
    x, y, z = (lax.axis_index(axis).astype(jnp.int32) for axis in ("dp", "y", "z"))
    pos = jnp.concatenate([jnp.stack([y, z, x]), lengths.reshape(pdev)])

    w_values = lax.all_gather(w_value, PSG, axis=0, tiled=True)
    gain = enc_gain[None]
    q_parts = call(
        query_kernel,
        shaped((answers, blocks, LANES)),
        [],
        pos,
        dec_states.reshape(answers, width),
        w_query,
        gain,
        hbm=(3,),
    )
    q_sum = call(spread_kernel, shaped(q_parts.shape), [], pos, exchange(q_parts))
    queries = exchange(q_sum)
    normed = normalise(
        pos, enc_states.reshape(slots, width), gain, min(slots, 128)
    )

    mine = lax.dynamic_slice(w_key, (0, x * quarter), (w_key.shape[0], quarter))
    keys = gather(mine, functools.partial(project, normed), normed, q_sum, queries)
    parts = call(
        functools.partial(attend_kernel, plen),
        shaped((answers, blocks + 1, LANES)),
        [
            pltpu.VMEM((NX, slots, quarter), bf16),
            pltpu.VMEM((pairs, slots), bf16),
            pltpu.VMEM((pairs, slots), bf16),
            pltpu.VMEM((answers, LANES), f32),
            pltpu.VMEM((slots, width), bf16),
            pltpu.VMEM((width, columns), bf16),
            pltpu.VMEM((slots, columns), f32),
            pltpu.SemaphoreType.DMA((NX,)),
            pltpu.SemaphoreType.DMA((PARTS,)),
            pltpu.SemaphoreType.DMA((len(ORDER),)),
        ],
        pos,
        queries,
        *keys,
        normed,
        w_values,
        mib=52,
        flops=2 * slots * width * columns,
        hbm=tuple(range(2, 4 + NX)),
    )
    rows = 2 * blocks
    merged = call(
        functools.partial(merge_kernel, pdev),
        shaped((members, rows, LANES), bf16),
        [pltpu.VMEM((members, rows, LANES), f32)],
        pos,
        exchange(parts),
    )
    part = call(
        out_kernel,
        shaped((answers + 8, w_out.shape[1])),
        [pltpu.VMEM((answers, rows, LANES), f32)],
        pos,
        exchange(merged),
        w_out,
    )
    other = lax.ppermute(part, "tp", [(0, 1), (1, 0)])
    attended, scores = call(
        functools.partial(last_kernel, pdev * members / (HEADS * answers)),
        [shaped((answers, w_out.shape[1]), bf16), shaped((1, pdev))],
        [],
        pos,
        part,
        other,
    )
    return attended[None], scores


def solution(mesh):
    fine = Mesh(mesh.devices.reshape(NX, NY, NZ, 2), ("dp", "y", "z", "tp"))
    placed = (
        P("dp", PSG, None, None),
        P("dp", PSG),
        P(),
        P("dp", None, None),
        P(PSG, "tp"),
        P(PSG, "tp"),
        P(PSG, "tp"),
        P("tp", PSG),
    )
    return jax.shard_map(
        body,
        mesh=fine,
        in_specs=placed,
        out_specs=(P("dp", None, PSG), P("dp", PSG)),
        check_vma=False,
    )
```
